256 devices in a mesh: kpt: 32 (over x, y, core), vir: 8 (over z).
Axes of the slice: x: 4, y: 4, z: 8, core: 2. Of those that a mesh axis runs over, the one named last changes fastest.
Arguments:
- df_pieces: bfloat16 [32, 32, 32, 4096], P('kpt', None, None, 'vir'), may hold values from -0.1875 to 0.1875
- amplitudes: bfloat16 [2, 4, 256, 4096], P(None, None, None, 'kpt'), may hold values from -6 to 6
- rest_residual: bfloat16 [32, 64, 64, 256], P('kpt', 'vir'), may hold values from -6 to 6
- occ_energy: bfloat16 [2, 16], replicated, may hold values from -2 to -0.29882812
- vir_energy: bfloat16 [32, 64], P('kpt'), may hold values from 0.29882812 to 3
- live_slots: int32 [32], P('kpt'), may hold values from 1 to 4, as said below
- mirror_slot: int32 [32, 4], P('kpt'), may hold values from 0 to 3, as said below
Outputs:
- amplitude_update: bfloat16 [32, 64, 64, 256], P('kpt', 'vir')
The draws below stay inside these ranges and needn't reach their ends.
Inputs may be any that keep to these rules, and one draw needn't show every extreme that they name: Slots r below live_slots[g] count in block g's sum; a block and its mirror block have equal values, and some block has 4. `mirror_slot`: row g maps each kc slot of block g to the slot of the mirror block that holds the same pair of k-points: a permutation of 0 to 3 that keeps slots below live_slots[g] below it; the mirror block's row is its inverse.
All inputs are finite; a program needn't handle non-finite values.
Results may differ from the reference program's by a relative error of at most 0.0043.
Values may be sent and summed in bfloat16 or wider, within the bound.
A program may use at most 128 MiB of HBM per device.

```python
import jax
import jax.numpy as jnp

NO = 16
NV = 64
NAUX = 256
KC = 4
NBLK = 32
AUXP = 32


def order_row(sub_key):
    return jax.random.permutation(sub_key, KC)


def slot_tables(key):
    half_blocks = NBLK // 2
    key_extra, key_keep, key_full, key_order = jax.random.split(key, 4)
    extra_slots = jax.random.randint(key_extra, (half_blocks,), 0, KC)
    keep_flag = jax.random.randint(key_keep, (half_blocks,), 0, 2)
    counts = 1 + extra_slots * keep_flag
    fullest = jax.random.randint(key_full, (), 0, half_blocks)
    counts = jnp.where(jnp.arange(half_blocks) == fullest, KC, counts).astype(jnp.int32)
    order_keys = jax.random.split(key_order, half_blocks)
    rank_rows = jax.vmap(order_row)(order_keys).astype(jnp.int32)
    scores = rank_rows + KC * (jnp.arange(KC)[None, :] >= counts[:, None]).astype(jnp.int32)
    forward = jnp.argsort(scores, axis=1).astype(jnp.int32)
    backward = jnp.argsort(forward, axis=1).astype(jnp.int32)
    return (jnp.concatenate([counts, counts]), jnp.concatenate([forward, backward], axis=0))


def draw_live_slots(key, part):
    return slot_tables(key)[0]


def draw_mirror_slot(key, part):
    return slot_tables(key)[1]


def block_scale(rng, dims, cuts, smallest, high):
    factor_of, own = 1.0, jax.random.fold_in(rng, 6)
    for position, blocks in cuts:
        draws = jnp.exp(jax.random.uniform(jax.random.fold_in(own, position), (blocks,), jnp.float32, smallest / len(cuts), high / len(cuts)))
        factor_of = factor_of * jnp.repeat(draws, dims[position] // blocks).reshape([-1 if axis == position else 1 for axis in range(len(dims))])
    return factor_of


def centred(stream_key, shape, deviation, limit, shards=(), held_as=jnp.bfloat16):
    array = jax.random.normal(stream_key, shape, jnp.float32) * deviation
    if len(shards) > 0:
        array = block_scale(stream_key, shape, shards, -0.22, 0.18) * array
    return jnp.clip(array, min=-limit, max=limit).astype(held_as)


def setup_inputs(seed: int = 0) -> dict:
    arg_keys = jax.random.split(jax.random.key(seed), 8)
    df_pieces = centred(arg_keys[0], (NBLK, NBLK, AUXP, NV * NV), 0.03125, 0.1875, ((0, 32), (3, 8)))
    amplitudes = centred(arg_keys[1], (2, KC, NO * NO, NV * NV), 1.0, 6.0, ((3, 32),))
    rest_residual = centred(arg_keys[2], (NBLK, NV, NV, NO * NO), 1.0, 6.0, ((0, 32), (1, 8)))
    occ_energy = jnp.clip(jax.random.uniform(arg_keys[3], (2, NO), jnp.float32, -2.0, -0.29882812), -2.0, -0.29882812).astype(jnp.bfloat16)
    vir_energy = jnp.clip(0.29882812 + 2.7011719 * jax.random.uniform(arg_keys[4], (NBLK, NV), jnp.float32) ** block_scale(arg_keys[4], (NBLK, NV), ((0, 32),), -0.2, 0.2), 0.29882812, 3.0).astype(jnp.bfloat16)
    live_slots = draw_live_slots(jax.random.fold_in(arg_keys[7], 71), 0)
    mirror_slot = draw_mirror_slot(jax.random.fold_in(arg_keys[7], 71), 0)
    return {"df_pieces": df_pieces, "amplitudes": amplitudes, "rest_residual": rest_residual, "occ_energy": occ_energy, "vir_energy": vir_energy, "live_slots": live_slots, "mirror_slot": mirror_slot}


def slab_of(df_pieces, block_index, slot_index):
    column = df_pieces[:, block_index].reshape(NAUX // AUXP, KC, AUXP, NV * NV)
    return jnp.take(column, slot_index, axis=1).reshape(NAUX, NV * NV)


def reference(df_pieces, amplitudes, rest_residual, occ_energy, vir_energy, live_slots, mirror_slot):
    half_blocks = NBLK // 2
    summed_list = []
    for block_index in range(NBLK):
        mirror_index = (block_index + half_blocks) % NBLK
        orient = block_index // half_blocks
        ladder = jnp.zeros((NV, NV, NO * NO), jnp.float32)
        for slot_index in range(KC):
            left_slab = slab_of(df_pieces, block_index, slot_index)
            right_slab = slab_of(df_pieces, mirror_index, mirror_slot[block_index, slot_index])
            pair_sums = jnp.dot(left_slab.T, right_slab, preferred_element_type=jnp.float32)
            coupling = pair_sums.astype(jnp.bfloat16).reshape(NV, NV, NV, NV)
            amp_block = amplitudes[orient, slot_index].reshape(NO * NO, NV, NV)
            ladder_term = jnp.einsum("acbd,icd->abi", coupling.astype(jnp.float32), amp_block.astype(jnp.float32))
            live_flag = (slot_index < live_slots[block_index]).astype(jnp.float32)
            ladder = ladder + live_flag * ladder_term
        summed_list.append(rest_residual[block_index].astype(jnp.float32) + ladder)
    occ_values = occ_energy.astype(jnp.float32)
    vir_values = vir_energy.astype(jnp.float32)
    results = []
    for block_index in range(NBLK):
        mirror_index = (block_index + half_blocks) % NBLK
        orient = block_index // half_blocks
        flipped = jnp.transpose(summed_list[mirror_index].reshape(NV, NV, NO, NO), (1, 0, 3, 2))
        symmetric = summed_list[block_index].reshape(NV, NV, NO, NO) + flipped
        denominator = (occ_values[orient][None, None, :, None] + occ_values[1 - orient][None, None, None, :]
                       - vir_values[block_index][:, None, None, None] - vir_values[mirror_index][None, :, None, None])
        results.append((symmetric / denominator).astype(jnp.bfloat16).reshape(NV, NV, NO * NO))
    return jnp.stack(results)
```

```python
import jax
import jax.numpy as jnp
from jax import lax
from jax.experimental import pallas as pl
from jax.experimental.pallas import tpu as pltpu
from jax.sharding import PartitionSpec as P

MESH = pl.DeviceIdType.MESH
ANY = pl.BlockSpec(memory_space=pl.ANY)
BF16 = jnp.bfloat16
F32 = jnp.float32
KPT = 32
VIR = 8
HALF = 16
VMEM_LIMIT = 56 * 1024 * 1024


def remote(src, dst, send, recv, device):
    return pltpu.make_async_remote_copy(
        src_ref=src, dst_ref=dst, send_sem=send, recv_sem=recv, device_id=device, device_id_type=MESH
    )


def signal(sem, device):
    pl.semaphore_signal(sem, inc=1, device_id=device, device_id_type=MESH)


def loop(low, high, body):
    def step(index, carry):
        body(index)
        return carry

    lax.fori_loop(low, high, step, 0)


def scatter_kernel(
    left_ref, right_ref, amp_ref, rest_ref, slab_ref, far_ref, got_ref, mirror_ref,
    own_sem, send_sem, recv_sem, rest_send, rest_recv,
):
    me = lax.axis_index("kpt")
    tile = lax.axis_index("vir")
    mirror = lax.rem(me + HALF, KPT)
    barrier = pltpu.get_barrier_semaphore()
    loop(1, KPT, lambda i: signal(barrier, (lax.rem(me + i, KPT), tile)))
    loop(1, VIR, lambda i: signal(barrier, (mirror, lax.rem(tile + i, VIR))))
    pl.semaphore_wait(barrier, KPT - 1 + VIR - 1)

    def parts(source, to):
        pair = to % HALF
        half = to // HALF
        rows = pl.ds((source // 4) * 32, 32)
        slot = source % 4
        return (
            (left_ref.at[pair], slab_ref.at[slot, rows]),
            (right_ref.at[half, pair], far_ref.at[slot, rows]),
            (amp_ref.at[to], got_ref.at[source]),
        )

    def copies(source, to):
        return [
            remote(src, dst, send_sem.at[kind, to], recv_sem.at[kind, source], (to, tile))
            for kind, (src, dst) in enumerate(parts(source, to))
        ]

    def rest_copy(source, to):
        return remote(
            rest_ref.at[to], mirror_ref.at[source], rest_send.at[to], rest_recv.at[source], (mirror, to)
        )

    def start(i):
        for copy in copies(me, lax.rem(me + i, KPT)):
            copy.start()

    loop(1, KPT, start)
    own = [
        pltpu.make_async_copy(src, dst, own_sem.at[kind])
        for kind, (src, dst) in enumerate(parts(me, me))
    ]
    for copy in own:
        copy.start()
    loop(0, VIR, lambda i: rest_copy(tile, lax.rem(tile + i, VIR)).start())

    def finish(i):
        other = lax.rem(me + KPT - i, KPT)
        for copy in copies(other, me):
            copy.wait_recv()
        for copy in copies(me, lax.rem(me + i, KPT)):
            copy.wait_send()

    loop(1, KPT, finish)

    def finish_rest(i):
        rest_copy(lax.rem(tile + VIR - i, VIR), tile).wait_recv()
        rest_copy(tile, lax.rem(tile + i, VIR)).wait_send()

    loop(0, VIR, finish_rest)
    for copy in own:
        copy.wait()


def scatter(left, right, amp, rest):
    return pl.pallas_call(
        scatter_kernel,
        out_shape=[
            jax.ShapeDtypeStruct((4, 256, 512), BF16),
            jax.ShapeDtypeStruct((4, 256, 256), BF16),
            jax.ShapeDtypeStruct((KPT, 16, 256), BF16),
            jax.ShapeDtypeStruct((VIR, 64, 256), BF16),
        ],
        in_specs=[ANY] * 4,
        out_specs=[ANY] * 4,
        scratch_shapes=[
            pltpu.SemaphoreType.DMA((3,)),
            pltpu.SemaphoreType.DMA((3, KPT)),
            pltpu.SemaphoreType.DMA((3, KPT)),
            pltpu.SemaphoreType.DMA((VIR,)),
            pltpu.SemaphoreType.DMA((VIR,)),
        ],
        compiler_params=pltpu.CompilerParams(collective_id=0, has_side_effects=True),
        name="scatter",
    )(left, right, amp, rest)


def gather_kernel(
    tile_ref, amp_ref, tiles_ref, amps_ref,
    own_sem, ring_send, ring_recv, amp_send, amp_recv, mate_send, mate_recv,
):
    me = lax.axis_index("kpt")
    z = lax.axis_index("vir")
    core = me % 2
    y = (me // 2) % 4
    x = me // 8
    x_near = x + 1 - 2 * (x % 2)

    def kpt(xx, yy, cc):
        return (xx * 4 + yy) * 2 + cc

    up = (y + 1) % 4
    down = (y + 3) % 4
    far = (y + 2) % 4
    mate = (kpt(x, y, 1 - core), z)
    side = (kpt(x_near, y, core), z)
    above = (kpt(x, up, core), z)
    below = (kpt(x, down, core), z)
    right = (me, lax.rem(z + 1, VIR))
    left = (me, lax.rem(z + VIR - 1, VIR))

    barrier = pltpu.get_barrier_semaphore()
    for device in (mate, side, above, below, right, left):
        signal(barrier, device)
    pl.semaphore_wait(barrier, 6)

    def place(xx, yy, cc):
        return ((xx % 2) * 4 + yy) * 2 + cc

    def ring(way, hop, slot):
        shift = VIR - hop if way == 0 else hop
        held = lax.rem(z + shift, VIR)
        source = tile_ref.at[slot] if hop == 0 else tiles_ref.at[held, slot]
        return remote(
            source, tiles_ref.at[held, slot], ring_send.at[way, hop, slot],
            ring_recv.at[way, hop, slot], right if way == 0 else left,
        )

    def ring_wait(way, hop, slot):
        shift = VIR - hop - 1 if way == 0 else hop + 1
        held = lax.rem(z + shift, VIR)
        remote(
            tile_ref.at[slot], tiles_ref.at[held, slot], ring_send.at[way, hop, slot],
            ring_recv.at[way, hop, slot], right if way == 0 else left,
        ).wait_recv()

    def hop_slots(way, hop):
        if hop < 3:
            return (0, 1, 2, 3)
        return (0, 1) if way == 0 else (2, 3)

    whole, first, second = pl.ds(0, 8), pl.ds(0, 4), pl.ds(4, 4)
    plan = (
        ((x, y), whole, above), ((x, y), whole, below), ((x, y), whole, side),
        ((x_near, y), whole, above), ((x_near, y), whole, below),
        ((x, down), first, above), ((x, up), second, below), ((x, far), whole, side),
    )
    arrive = (
        ((x, down), whole), ((x, up), whole), ((x_near, y), whole),
        ((x_near, down), whole), ((x_near, up), whole),
        ((x, far), first), ((x, far), second), ((x_near, far), whole),
    )

    def amp_copy(number):
        (xx, yy), part, device = plan[number]
        spot = amps_ref.at[place(xx, yy, core), part]
        source = amp_ref.at[part] if number < 3 else spot
        return remote(source, spot, amp_send.at[number], amp_recv.at[number], device)

    def amp_wait(number):
        (xx, yy), part = arrive[number]
        spot = amps_ref.at[place(xx, yy, core), part]
        remote(spot, spot, amp_send.at[number], amp_recv.at[number], mate).wait_recv()

    def mate_copy(number, xx, yy, part, source=None):
        spot = amps_ref.at[place(xx, yy, core), part]
        return remote(
            spot if source is None else source, spot, mate_send.at[number], mate_recv.at[number], mate
        )

    def mate_wait(number, xx, yy, part):
        spot = amps_ref.at[place(xx, yy, 1 - core), part]
        remote(spot, spot, mate_send.at[number], mate_recv.at[number], mate).wait_recv()

    started = []

    def go(copy):
        copy.start()
        started.append(copy)

    for number in range(3):
        go(amp_copy(number))
    for slot in range(4):
        go(ring(0, 0, slot))
        go(ring(1, 0, slot))
    go(mate_copy(8, x, y, whole, amp_ref))
    own_amp = pltpu.make_async_copy(amp_ref, amps_ref.at[place(x, y, core)], own_sem.at[0])
    own_tile = pltpu.make_async_copy(tile_ref, tiles_ref.at[z], own_sem.at[1])
    own_amp.start()
    own_tile.start()

    def ring_step(hop):
        for slot in range(4):
            for way in (0, 1):
                if slot in hop_slots(way, hop):
                    ring_wait(way, hop, slot)
                    if hop < 3 and slot in hop_slots(way, hop + 1):
                        go(ring(way, hop + 1, slot))

    def amp_step(number, forward):
        amp_wait(number)
        for other in forward:
            go(amp_copy(other))
        (xx, yy), part = arrive[number]
        go(mate_copy(number, xx, yy, part))

    amp_step(2, (3, 4))
    amp_step(0, (5,))
    amp_step(1, (6,))
    ring_step(0)
    amp_wait(5)
    amp_wait(6)
    go(amp_copy(7))
    go(mate_copy(5, x, far, first))
    go(mate_copy(6, x, far, second))
    ring_step(1)
    amp_step(3, ())
    amp_step(4, ())
    ring_step(2)
    amp_step(7, ())
    ring_step(3)
    for number in range(8):
        (xx, yy), part = arrive[number]
        mate_wait(number, xx, yy, part)
    mate_wait(8, x, y, whole)
    for copy in started:
        copy.wait_send()
    own_amp.wait()
    own_tile.wait()


def gather(tile, amp):
    return pl.pallas_call(
        gather_kernel,
        out_shape=[
            jax.ShapeDtypeStruct((VIR, 4, 256, 256), BF16),
            jax.ShapeDtypeStruct((HALF, 8, 128, 256), BF16),
        ],
        in_specs=[ANY] * 2,
        out_specs=[ANY] * 2,
        scratch_shapes=[
            pltpu.SemaphoreType.DMA((2,)),
            pltpu.SemaphoreType.DMA((2, 4, 4)),
            pltpu.SemaphoreType.DMA((2, 4, 4)),
            pltpu.SemaphoreType.DMA((8,)),
            pltpu.SemaphoreType.DMA((8,)),
            pltpu.SemaphoreType.DMA((9,)),
            pltpu.SemaphoreType.DMA((9,)),
        ],
        compiler_params=pltpu.CompilerParams(collective_id=1, has_side_effects=True),
        name="gather",
    )(tile, amp)


def ladder_kernel(slots_ref, live_ref, slab_ref, tiles_ref, near_ref, far_ref, out_ref, lhs, total):
    slot = pl.program_id(0)

    @pl.when(slot == 0)
    def _():
        total[...] = jnp.zeros_like(total)

    @pl.when(slot < live_ref[0])
    def _():
        low = lax.broadcasted_iota(jnp.int32, (VIR, 8, 128), 2) < 64

        def chunk(index):
            rows = tiles_ref[:, 0, pl.ds(pl.multiple_of(index * 32, 32), 32), :].reshape(256, 256)
            coupling = jnp.dot(rows, slab_ref[0], preferred_element_type=F32).reshape(VIR, 4, 8, 512)
            for pair in range(4):
                part = coupling[..., pair * 128 : (pair + 1) * 128]
                evens, odds = [], []
                for first in (0, 2):
                    here, there = part[:, first], part[:, first + 1]
                    evens.append(jnp.where(low, here, pltpu.roll(there, 64, 2)))
                    odds.append(jnp.where(low, pltpu.roll(here, 64, 2), there))
                block = jnp.concatenate(
                    [jnp.concatenate(evens, axis=2), jnp.concatenate(odds, axis=2)], axis=1
                )
                lhs[:, pair * 16 : (pair + 1) * 16, :] = block.astype(BF16)
            two = pl.ds(index * 2, 2)
            amps = near_ref[two, 0].astype(F32) + far_ref[two, 0].astype(F32)
            total[...] += jnp.dot(
                lhs[...].reshape(512, 256), amps.astype(BF16).reshape(256, 256), preferred_element_type=F32
            )

        loop(0, 8, chunk)

    @pl.when(slot == 3)
    def _():
        out_ref[...] = total[...].astype(BF16).reshape(VIR, 64, 256)


def ladder(slots, live, slab, tiles, amps):
    return pl.pallas_call(
        ladder_kernel,
        out_shape=jax.ShapeDtypeStruct((VIR, 64, 256), BF16),
        grid_spec=pltpu.PrefetchScalarGridSpec(
            num_scalar_prefetch=2,
            grid=(4,),
            in_specs=[
                pl.BlockSpec((1, 256, 512), lambda r, m, n: (r, 0, 0)),
                pl.BlockSpec((VIR, 1, 256, 256), lambda r, m, n: (0, m[r], 0, 0)),
                pl.BlockSpec((HALF, 1, 128, 256), lambda r, m, n: (0, r, 0, 0)),
                pl.BlockSpec((HALF, 1, 128, 256), lambda r, m, n: (0, m[r] + 4, 0, 0)),
            ],
            out_specs=pl.BlockSpec((VIR, 64, 256), lambda r, m, n: (0, 0, 0)),
            scratch_shapes=[pltpu.VMEM((VIR, 64, 256), BF16), pltpu.VMEM((512, 256), F32)],
        ),
        compiler_params=pltpu.CompilerParams(vmem_limit_bytes=VMEM_LIMIT),
        cost_estimate=pl.CostEstimate(flops=4_300_000_000, bytes_accessed=14_000_000, transcendentals=0),
        name="ladder",
    )(slots, live, slab, tiles, amps, amps)


def exchange_kernel(part_ref, got_ref, own_sem, send_sem, recv_sem):
    me = lax.axis_index("kpt")
    z = lax.axis_index("vir")
    half = me // HALF
    mirror = lax.rem(me + HALF, KPT)
    barrier = pltpu.get_barrier_semaphore()
    loop(0, VIR, lambda i: signal(barrier, (mirror, lax.rem(z + i, VIR))))
    loop(1, VIR, lambda i: signal(barrier, (me, lax.rem(z + i, VIR))))
    pl.semaphore_wait(barrier, 2 * VIR - 1)

    def piece(kind, source, to, device):
        return remote(
            part_ref.at[to], got_ref.at[kind, source], send_sem.at[kind, to], recv_sem.at[kind, source],
            (device, to),
        )

    @pl.when(half == 0)
    def _():
        whole = remote(part_ref, got_ref.at[0], send_sem.at[2, 0], recv_sem.at[2, 0], (mirror, z))
        loop(0, VIR, lambda i: piece(0, z, lax.rem(z + i, VIR), mirror).start())
        whole.wait_recv()
        loop(0, VIR, lambda i: piece(0, z, lax.rem(z + i, VIR), mirror).wait_send())

    @pl.when(half == 1)
    def _():
        whole = remote(part_ref, got_ref.at[0], send_sem.at[2, 0], recv_sem.at[2, 0], (mirror, z))
        own = pltpu.make_async_copy(part_ref.at[z], got_ref.at[1, z], own_sem)
        whole.start()
        own.start()
        loop(1, VIR, lambda i: piece(1, z, lax.rem(z + i, VIR), me).start())
        loop(0, VIR, lambda i: piece(0, lax.rem(z + i, VIR), z, me).wait_recv())
        loop(1, VIR, lambda i: piece(1, lax.rem(z + i, VIR), z, me).wait_recv())
        loop(1, VIR, lambda i: piece(1, z, lax.rem(z + i, VIR), me).wait_send())
        whole.wait_send()
        own.wait()


def exchange(part):
    return pl.pallas_call(
        exchange_kernel,
        out_shape=jax.ShapeDtypeStruct((2, VIR, 64, 256), BF16),
        in_specs=[ANY],
        out_specs=ANY,
        scratch_shapes=[
            pltpu.SemaphoreType.DMA,
            pltpu.SemaphoreType.DMA((3, VIR)),
            pltpu.SemaphoreType.DMA((3, VIR)),
        ],
        compiler_params=pltpu.CompilerParams(collective_id=2, has_side_effects=True),
        name="exchange",
    )(part)


def one_hot(targets, count):
    return (targets[:, None] == jnp.arange(count)[None, :]).astype(BF16)


def pick(spec, left, right):
    return jnp.einsum(spec, left, right, preferred_element_type=F32).astype(BF16)


def shards(df_pieces, amplitudes, rest_residual, occ_energy, vir_energy, live_slots, mirror_slot):
    me = lax.axis_index("kpt")
    z = lax.axis_index("vir")
    half = me // HALF
    far_energy = lax.ppermute(vir_energy, "kpt", [(s, (s + HALF) % KPT) for s in range(KPT)])

    lane = jnp.arange(512)
    b, d = lane // 64, lane % 64
    by_half = one_hot((d // 32) * 256 + (d % 32) * 8 + b, 512).reshape(512, 2, 256)
    left = df_pieces[0, :HALF]
    right = pick("gak,khn->hgan", df_pieces[0, HALF:], by_half)
    k = jnp.arange(128)
    c2, owner, d2 = k // 64, (k % 64) // 2, k % 2
    order = one_hot(owner * 4 + d2 * 2 + c2, 128)
    send_amp = pick("rnk,kl->rln", amplitudes[0], order)
    send_amp = send_amp.reshape(4, KPT, 4, 256).transpose(1, 0, 2, 3).reshape(KPT, 16, 256)
    n = jnp.arange(256)
    swap = one_hot((n % 16) * 16 + n // 16, 256)
    amp_one = pick("rnk,nm->rkm", amplitudes[1], swap)
    send_rest = rest_residual[0].reshape(8, VIR, 8, 256).transpose(1, 0, 2, 3).reshape(VIR, 64, 256)

    slab, far, got, mirror_rest = scatter(left, right, send_amp, send_rest)

    far = jnp.swapaxes(far, 1, 2)
    m = jnp.arange(512)
    p, r, e2, f2 = m // 16, (m % 16) // 4, (m % 4) // 2, m % 2
    regroup = one_hot(r * 128 + e2 * 64 + p * 2 + f2, 512)
    amp_zero = pick("mo,mn->on", regroup, got.reshape(512, 256)).reshape(4, 128, 256)
    tiles, amps = gather(far, jnp.concatenate([amp_zero, amp_one], axis=0))

    row = mirror_slot[0]
    inverse = jnp.sum(
        jnp.where(row[None, :] == jnp.arange(4)[:, None], jnp.arange(4)[None, :], 0), axis=1
    ).astype(jnp.int32)
    slots = jnp.where(half == 0, row, inverse)
    part = ladder(slots, live_slots, slab, tiles, amps)
    shared = exchange(part)

    forward = half == 0
    zero = jnp.zeros((), BF16)
    flipped = jnp.concatenate(
        [
            mirror_rest.reshape(512, 256),
            jnp.where(forward, zero, shared[0]).reshape(512, 256),
            jnp.where(forward, zero, shared[1]).reshape(512, 256),
        ],
        axis=1,
    )
    flipped = jnp.dot(flipped, jnp.concatenate([swap] * 3, axis=0), preferred_element_type=F32)
    flipped = flipped.reshape(VIR, 8, 8, 256).transpose(2, 0, 1, 3)
    direct = jnp.where(forward, part.astype(F32) + shared[0].astype(F32), 0.0)
    direct = direct.reshape(VIR, 8, 8, 256).transpose(1, 0, 2, 3)
    summed = rest_residual[0].astype(F32) + direct.reshape(8, 64, 256)
    symmetric = summed + flipped.reshape(8, 64, 256)

    occ = occ_energy.astype(F32)
    occ_first = lax.dynamic_index_in_dim(occ, half, 0, keepdims=False)
    occ_second = lax.dynamic_index_in_dim(occ, 1 - half, 0, keepdims=False)
    occ_pair = (occ_first[:, None] + occ_second[None, :]).reshape(256)
    own_vir = lax.dynamic_slice_in_dim(vir_energy[0].astype(F32), z * 8, 8)
    far_vir = far_energy[0].astype(F32)
    denominator = occ_pair[None, None, :] - own_vir[:, None, None] - far_vir[None, :, None]
    return (symmetric / denominator).astype(BF16)[None]


def solution(mesh):
    placed = (
        P("kpt", None, None, "vir"),
        P(None, None, None, "kpt"),
        P("kpt", "vir", None, None),
        P(),
        P("kpt", None),
        P("kpt"),
        P("kpt", None),
    )
    return jax.shard_map(
        shards, mesh=mesh, in_specs=placed, out_specs=P("kpt", "vir", None, None), check_vma=False
    )
```

```python
import jax
import jax.numpy as jnp
from jax import lax
from jax.experimental import pallas as pl
from jax.experimental.pallas import tpu as pltpu
from jax.sharding import PartitionSpec as P

MESH = pl.DeviceIdType.MESH
BF16 = jnp.bfloat16
F32 = jnp.float32
KPT = 32
VIR = 8
HALF = 16


def remote(src, dst, send, recv, device):
    return pltpu.make_async_remote_copy(
        src_ref=src, dst_ref=dst, send_sem=send, recv_sem=recv, device_id=device, device_id_type=MESH
    )


def signal(sem, device):
    pl.semaphore_signal(sem, inc=1, device_id=device, device_id_type=MESH)


def loop(low, high, body):
    def step(index, carry):
        body(index)
        return carry

    lax.fori_loop(low, high, step, 0)


def one_hot(rows, columns, target):
    row = lax.broadcasted_iota(jnp.int32, (rows, columns), 0)
    column = lax.broadcasted_iota(jnp.int32, (rows, columns), 1)
    return jnp.where(target(row) == column, 1.0, 0.0).astype(BF16)


def dot(left, right):
    return jnp.dot(left, right, preferred_element_type=F32)


def dot_rows(left, right):
    return lax.dot_general(left, right, (((1,), (1,)), ((), ())), preferred_element_type=F32)


def bits(value, low, count):
    return (value >> low) & ((1 << count) - 1)


def fused_kernel(
    slots_ref, live_ref, df_ref, amp_ref, rest_ref, energy_ref, occ_ref, out_ref,
    raw, right, chunk, far, slab, got, srest, mrest, senergy, menergy,
    tiles, amps, coupled, total, part, shared,
    own_sem, send_sem, recv_sem, rest_send, rest_recv, ring_send, ring_recv,
    amp_send, amp_recv, mate_send, mate_recv, swap_send, swap_recv,
):
    me = lax.axis_index("kpt")
    z = lax.axis_index("vir")
    half = me // HALF
    mirror = lax.rem(me + HALF, KPT)
    core = me % 2
    y = (me // 2) % 4
    x = me // 8
    x_near = x + 1 - 2 * (x % 2)

    def kpt(xx, yy, cc):
        return (xx * 4 + yy) * 2 + cc

    up, down, opposite = (y + 1) % 4, (y + 3) % 4, (y + 2) % 4
    mate = (kpt(x, y, 1 - core), z)
    side = (kpt(x_near, y, core), z)
    above = (kpt(x, up, core), z)
    below = (kpt(x, down, core), z)
    ahead = (me, lax.rem(z + 1, VIR))
    behind = (me, lax.rem(z + VIR - 1, VIR))

    def place(xx, yy, cc):
        return ((xx % 2) * 4 + yy) * 2 + cc

    spot_me = place(x, y, core)

    load = pltpu.make_async_copy(df_ref.at[pl.ds(HALF, HALF)], raw, own_sem.at[4])
    load.start()
    barrier = pltpu.get_barrier_semaphore()
    loop(1, KPT, lambda i: signal(barrier, (lax.rem(me + i, KPT), z)))
    loop(1, VIR, lambda i: signal(barrier, (mirror, lax.rem(z + i, VIR))))
    loop(1, VIR, lambda i: signal(barrier, (me, lax.rem(z + i, VIR))))

    by_half = one_hot(
        512, 512, lambda n: bits(n, 5, 1) * 256 + bits(n, 0, 5) * 8 + bits(n, 6, 3)
    )
    load.wait()
    for side_half in range(2):
        picked = dot(raw[...].reshape(512, 512), by_half[:, side_half * 256 : side_half * 256 + 256])
        right[side_half] = picked.astype(BF16).reshape(HALF, 32, 256)

    pl.semaphore_wait(barrier, KPT - 1 + 2 * (VIR - 1))

    def spread(kind, source, to):
        pair = to % HALF
        rows = pl.ds(pl.multiple_of((source // 4) * 32, 32), 32)
        slot = source % 4
        if kind == 0:
            return right.at[to // HALF, pair], far.at[slot, rows]
        if kind == 1:
            return chunk.at[to], got.at[source]
        return df_ref.at[pair], slab.at[slot, rows]

    def spread_copy(kind, source, to):
        src, dst = spread(kind, source, to)
        return remote(src, dst, send_sem.at[kind, to], recv_sem.at[kind, source], (to, z))

    def own_spread(kind):
        src, dst = spread(kind, me, me)
        return pltpu.make_async_copy(src, dst, own_sem.at[kind])

    def spread_start(kind):
        loop(1, KPT, lambda i: spread_copy(kind, me, lax.rem(me + i, KPT)).start())
        own_spread(kind).start()

    def spread_recv(kind):
        loop(1, KPT, lambda i: spread_copy(kind, lax.rem(me + KPT - i, KPT), me).wait_recv())
        own_spread(kind).wait()

    def spread_sent(kind):
        loop(1, KPT, lambda i: spread_copy(kind, me, lax.rem(me + i, KPT)).wait_send())

    spread_start(0)

    order = one_hot(
        128, 128, lambda n: bits(n, 6, 1) * 64 + bits(n, 0, 6)
    )
    lined = jnp.concatenate(
        [dot_rows(order, amp_ref[0, slot]).astype(BF16) for slot in range(4)], axis=0
    )
    to_owner = one_hot(
        512, 512,
        lambda n: bits(n, 2, 2) * 128 + bits(n, 0, 1) * 64 + bits(n, 4, 5) * 2 + bits(n, 1, 1),
    )
    chunk[...] = dot(to_owner, lined).astype(BF16).reshape(KPT, 16, 256)
    spread_start(1)
    spread_start(2)

    turn = one_hot(256, 256, lambda n: bits(n, 0, 4) * 16 + bits(n, 4, 4))
    for slot in range(4):
        turned = dot(turn, amp_ref[1, slot]).astype(BF16)
        amps[spot_me, 4 + slot] = dot_rows(order, turned).astype(BF16)

    plan = (
        ((x, y), 0, 4, above), ((x, y), 0, 4, below), ((x, y), 0, 4, side),
        ((x_near, y), 0, 4, above), ((x_near, y), 0, 4, below),
        ((x, down), 0, 2, above), ((x, up), 2, 2, below), ((x, opposite), 0, 4, side),
    )
    arrive = (
        ((x, down), 0, 4), ((x, up), 0, 4), ((x_near, y), 0, 4),
        ((x_near, down), 0, 4), ((x_near, up), 0, 4),
        ((x, opposite), 0, 2), ((x, opposite), 2, 2), ((x_near, opposite), 0, 4),
        ((x, y), 0, 4),
    )

    def amp_copy(group, number):
        (xx, yy), low, count, device = plan[number]
        spot = amps.at[place(xx, yy, core), pl.ds(group * 4 + low, count)]
        return remote(spot, spot, amp_send.at[group, number], amp_recv.at[group, number], device)

    def amp_wait(group, number):
        (xx, yy), low, count = arrive[number]
        spot = amps.at[place(xx, yy, core), pl.ds(group * 4 + low, count)]
        remote(spot, spot, amp_send.at[group, number], amp_recv.at[group, number], mate).wait_recv()

    def mate_copy(group, number, whose):
        (xx, yy), low, count = arrive[number]
        spot = amps.at[place(xx, yy, whose), pl.ds(group * 4 + low, count)]
        return remote(spot, spot, mate_send.at[group, number], mate_recv.at[group, number], mate)

    def amp_begin(group):
        for number in range(3):
            amp_copy(group, number).start()
        mate_copy(group, 8, core).start()

    def amp_steps(group, numbers, forward):
        for number in numbers:
            amp_wait(group, number)
        for number in forward:
            amp_copy(group, number).start()
        for number in numbers:
            mate_copy(group, number, core).start()

    amp_begin(1)

    rest = rest_ref[...].astype(F32)
    for tile in range(VIR):
        srest[tile] = rest[:, tile * 8 : tile * 8 + 8, :].reshape(64, 256).astype(BF16)

    def rest_copy(source, to):
        return remote(
            srest.at[to], mrest.at[source], rest_send.at[to], rest_recv.at[source], (mirror, to)
        )

    energy_copy = remote(
        senergy, menergy, rest_send.at[VIR], rest_recv.at[VIR], (mirror, z)
    )
    senergy[...] = energy_ref[...]
    loop(0, VIR, lambda i: rest_copy(z, lax.rem(z + i, VIR)).start())
    energy_copy.start()

    spread_recv(0)
    eye = one_hot(256, 256, lambda n: n)
    for slot in range(4):
        tiles[z, slot] = dot_rows(eye, far[slots_ref[slot]]).astype(BF16)

    def ring(way, hop, slot):
        held = lax.rem(z + (VIR - hop if way == 0 else hop), VIR)
        spot = tiles.at[held, slot]
        return remote(
            spot, spot, ring_send.at[way, hop, slot], ring_recv.at[way, hop, slot],
            ahead if way == 0 else behind,
        )

    def ring_wait(way, hop, slot):
        held = lax.rem(z + (VIR - hop - 1 if way == 0 else hop + 1), VIR)
        spot = tiles.at[held, slot]
        remote(
            spot, spot, ring_send.at[way, hop, slot], ring_recv.at[way, hop, slot],
            ahead if way == 0 else behind,
        ).wait_recv()

    def ways(hop, slot):
        if hop < 3:
            return (0, 1)
        return (0,) if slot < 2 else (1,)

    for slot in range(4):
        for way in (0, 1):
            ring(way, 0, slot).start()

    def ring_step(hop, slot):
        for way in ways(hop, slot):
            ring_wait(way, hop, slot)
        if hop < 3:
            for way in ways(hop + 1, slot):
                ring(way, hop + 1, slot).start()

    low = lax.broadcasted_iota(jnp.int32, (8, 8, 128), 2) < 64

    def couple(tile, slot):
        product = dot(tiles[tile, slot], slab[slot]).reshape(8, 4, 8, 512)
        for pair in range(4):
            piece = product[..., pair * 128 : (pair + 1) * 128]
            evens, odds = [], []
            for first in (0, 2):
                here, there = piece[:, first], piece[:, first + 1]
                evens.append(jnp.where(low, here, pltpu.roll(there, 64, 2)))
                odds.append(jnp.where(low, pltpu.roll(here, 64, 2), there))
            block = jnp.concatenate(
                [jnp.concatenate(evens, axis=2), jnp.concatenate(odds, axis=2)], axis=1
            )
            coupled[slot, :, tile, pair * 16 : (pair + 1) * 16, :] = block.astype(BF16)

    def couple_two(hop, slot):
        loop(0, 2, lambda i: couple(lax.rem(z + VIR + (2 * i - 1) * (hop + 1), VIR), slot))

    spread_recv(1)
    regroup = one_hot(
        512, 512,
        lambda n: bits(n, 1, 5) * 16 + bits(n, 7, 2) * 4 + bits(n, 6, 1) * 2 + bits(n, 0, 1),
    )
    regrouped = dot(regroup, got[...].reshape(512, 256)).astype(BF16)
    amps[spot_me, 0:4] = regrouped.reshape(4, 128, 256)
    amp_begin(0)

    for slot in range(4):
        ring_step(0, slot)
    spread_recv(2)
    for slot in range(4):
        ring_step(1, slot)
        couple(z, slot)
        couple_two(0, slot)
        if slot == 1:
            amp_steps(1, (2, 0, 1), (3, 4, 5, 6))
        if slot == 3:
            amp_steps(0, (2, 0, 1), (3, 4, 5, 6))
    for slot in range(4):
        ring_step(2, slot)
        couple_two(1, slot)
        if slot == 0:
            amp_steps(1, (5, 6), (7,))
        if slot == 2:
            amp_steps(0, (5, 6), (7,))
    amp_steps(1, (3, 4), ())
    for slot in range(4):
        ring_step(3, slot)
        couple_two(2, slot)
    amp_steps(0, (3, 4), ())
    loop(0, 4, lambda slot: couple(lax.rem(z + 4, VIR), slot))
    amp_steps(1, (7,), ())
    amp_steps(0, (7,), ())
    for group in range(2):
        for number in range(9):
            mate_copy(group, number, 1 - core).wait_recv()

    total[...] = jnp.zeros_like(total)

    def ladder(index):
        slot, block = index // 8, index % 8
        two = pl.ds(block * 2, 2)
        near = amps[two, slot].astype(F32)
        away = amps[two, 4 + slots_ref[slot]].astype(F32)
        both = jnp.where(slot < live_ref[0], near + away, 0.0).astype(BF16)
        total[...] += dot(coupled[slot, block].reshape(512, 256), both.reshape(256, 256))

    loop(0, 32, ladder)
    part[...] = total[...].astype(BF16).reshape(VIR, 64, 256)

    def piece_copy(kind, source, to, device):
        return remote(
            part.at[to], shared.at[kind, source], swap_send.at[kind, to], swap_recv.at[kind, source],
            (device, to),
        )

    whole = remote(part, shared.at[0], swap_send.at[2, 0], swap_recv.at[2, 0], (mirror, z))
    occ = occ_ref[...]

    def finish(direct, flipped):
        rows = one_hot(512, 512, lambda n: bits(n, 0, 6) * 8 + bits(n, 6, 3))
        summed = 0.0
        for block in flipped:
            moved = dot(rows, block.reshape(512, 256)).astype(BF16)
            summed = summed + dot(moved, turn)
        summed = summed.reshape(8, 64, 256)
        distant = jnp.concatenate([menergy[...]] * 2, axis=1)
        for v in range(8):
            value = rest_ref[v].astype(F32) + summed[v]
            if direct is not None:
                value = value + direct[:, v * 8 : v * 8 + 8, :].reshape(64, 256)
            near = jnp.concatenate([energy_ref[pl.ds(z * 8 + v, 1), :]] * 2, axis=1)
            out_ref[v] = (value / (occ - near - distant)).astype(BF16)

    loop(0, VIR, lambda i: rest_copy(lax.rem(z + i, VIR), z).wait_recv())
    energy_copy.wait_recv()

    @pl.when(half == 0)
    def _():
        loop(0, VIR, lambda i: piece_copy(0, z, lax.rem(z + i, VIR), mirror).start())
        whole.wait_recv()
        direct = total[...].reshape(VIR, 64, 256) + shared[0].astype(F32)
        finish(direct, (mrest[...],))
        loop(0, VIR, lambda i: piece_copy(0, z, lax.rem(z + i, VIR), mirror).wait_send())

    @pl.when(half == 1)
    def _():
        own = pltpu.make_async_copy(part.at[z], shared.at[1, z], own_sem.at[3])
        whole.start()
        own.start()
        loop(1, VIR, lambda i: piece_copy(1, z, lax.rem(z + i, VIR), me).start())
        loop(0, VIR, lambda i: piece_copy(0, lax.rem(z + i, VIR), z, me).wait_recv())
        loop(1, VIR, lambda i: piece_copy(1, lax.rem(z + i, VIR), z, me).wait_recv())
        own.wait()
        finish(None, (mrest[...], shared[0], shared[1]))
        loop(1, VIR, lambda i: piece_copy(1, z, lax.rem(z + i, VIR), me).wait_send())
        whole.wait_send()

    for kind in range(3):
        spread_sent(kind)
    loop(0, VIR, lambda i: rest_copy(z, lax.rem(z + i, VIR)).wait_send())
    energy_copy.wait_send()
    for slot in range(4):
        for hop in range(4):
            for way in ways(hop, slot):
                ring(way, hop, slot).wait_send()
    for group in range(2):
        for number in range(8):
            amp_copy(group, number).wait_send()
        for number in range(9):
            mate_copy(group, number, core).wait_send()


def fused(slots, live, df, amp, rest, energy, occ):
    vmem = pl.BlockSpec(memory_space=pltpu.VMEM)
    smem = pl.BlockSpec(memory_space=pltpu.SMEM)
    dma = pltpu.SemaphoreType.DMA
    return pl.pallas_call(
        fused_kernel,
        out_shape=jax.ShapeDtypeStruct((8, 64, 256), BF16),
        in_specs=[smem, smem, pl.BlockSpec(memory_space=pl.ANY), vmem, vmem, vmem, vmem],
        out_specs=vmem,
        scratch_shapes=[
            pltpu.VMEM((HALF, 32, 512), BF16),
            pltpu.VMEM((2, HALF, 32, 256), BF16),
            pltpu.VMEM((KPT, 16, 256), BF16),
            pltpu.VMEM((4, 256, 256), BF16),
            pltpu.VMEM((4, 256, 512), BF16),
            pltpu.VMEM((KPT, 16, 256), BF16),
            pltpu.VMEM((VIR, 64, 256), BF16),
            pltpu.VMEM((VIR, 64, 256), BF16),
            pltpu.VMEM((64, 128), F32),
            pltpu.VMEM((64, 128), F32),
            pltpu.VMEM((VIR, 4, 256, 256), BF16),
            pltpu.VMEM((HALF, 8, 128, 256), BF16),
            pltpu.VMEM((4, 8, VIR, 64, 256), BF16),
            pltpu.VMEM((512, 256), F32),
            pltpu.VMEM((VIR, 64, 256), BF16),
            pltpu.VMEM((2, VIR, 64, 256), BF16),
            dma((5,)),
            dma((3, KPT)),
            dma((3, KPT)),
            dma((VIR + 1,)),
            dma((VIR + 1,)),
            dma((2, 4, 4)),
            dma((2, 4, 4)),
            dma((2, 8)),
            dma((2, 8)),
            dma((2, 9)),
            dma((2, 9)),
            dma((3, VIR)),
            dma((3, VIR)),
        ],
        compiler_params=pltpu.CompilerParams(
            collective_id=0, has_side_effects=True, vmem_limit_bytes=56 * 1024 * 1024
        ),
        name="fused",
    )(slots, live, df, amp, rest, energy, occ)


def shards(df_pieces, amplitudes, rest_residual, occ_energy, vir_energy, live_slots, mirror_slot):
    half = lax.axis_index("kpt") // HALF
    row = mirror_slot[0]
    inverse = jnp.sum(
        jnp.where(row[None, :] == jnp.arange(4)[:, None], jnp.arange(4)[None, :], 0), axis=1
    ).astype(jnp.int32)
    slots = jnp.where(half == 0, row, inverse)
    occ = occ_energy.astype(F32)
    occ_first = lax.dynamic_index_in_dim(occ, half, 0, keepdims=False)
    occ_second = lax.dynamic_index_in_dim(occ, 1 - half, 0, keepdims=False)
    occ_pair = (occ_first[:, None] + occ_second[None, :]).reshape(1, 256)
    energy = jnp.broadcast_to(vir_energy[0].astype(F32)[:, None], (64, 128))
    out = fused(
        slots, live_slots, df_pieces[0], amplitudes, rest_residual[0], energy, occ_pair
    )
    return out[None]


def solution(mesh):
    placed = (
        P("kpt", None, None, "vir"),
        P(None, None, None, "kpt"),
        P("kpt", "vir", None, None),
        P(),
        P("kpt", None),
        P("kpt"),
        P("kpt", None),
    )
    return jax.shard_map(
        shards, mesh=mesh, in_specs=placed, out_specs=P("kpt", "vir", None, None), check_vma=False
    )
```

```python
import jax
import jax.numpy as jnp
from jax import lax
from jax.experimental import pallas as pl
from jax.experimental.pallas import tpu as pltpu
from jax.sharding import PartitionSpec as P

MESH = pl.DeviceIdType.MESH
BF16 = jnp.bfloat16
F32 = jnp.float32
KPT = 32
VIR = 8
HALF = 16


def remote(src, dst, send, recv, device):
    return pltpu.make_async_remote_copy(
        src_ref=src, dst_ref=dst, send_sem=send, recv_sem=recv, device_id=device, device_id_type=MESH
    )


def signal(sem, device):
    pl.semaphore_signal(sem, inc=1, device_id=device, device_id_type=MESH)


def loop(low, high, body):
    def step(index, carry):
        body(index)
        return carry

    lax.fori_loop(low, high, step, 0)


def one_hot(rows, columns, target):
    row = lax.broadcasted_iota(jnp.int32, (rows, columns), 0)
    column = lax.broadcasted_iota(jnp.int32, (rows, columns), 1)
    return jnp.where(target(row) == column, 1.0, 0.0).astype(BF16)


def dot(left, right):
    return jnp.dot(left, right, preferred_element_type=F32)


def dot_rows(left, right):
    return lax.dot_general(left, right, (((1,), (1,)), ((), ())), preferred_element_type=F32)


def bits(value, low, count):
    return (value >> low) & ((1 << count) - 1)


def fused_kernel(
    slots_ref, live_ref, df_ref, amp_hbm, rest_hbm, occ_ref, vir_ref, out_ref,
    raw, amp_ref, rest_ref, right, chunk, far, middle, slab, got, srest, mrest, senergy, menergy,
    tiles, amps, coupled, summed_amps, total, part, shared, mover, turner,
    own_sem, load_sem, send_sem, recv_sem, slab_send, slab_recv, rest_send, rest_recv,
    ring_send, ring_recv, amp_send, amp_recv, mate_send, mate_recv, swap_send, swap_recv,
):
    me = lax.axis_index("kpt")
    z = lax.axis_index("vir")
    half = me // HALF
    mirror = lax.rem(me + HALF, KPT)
    core = me % 2
    y = (me // 2) % 4
    x = me // 8
    x_near = x + 1 - 2 * (x % 2)

    def kpt(xx, yy, cc):
        return (xx * 4 + yy) * 2 + cc

    up, down, opposite = (y + 1) % 4, (y + 3) % 4, (y + 2) % 4
    mate = (kpt(x, y, 1 - core), z)
    side = (kpt(x_near, y, core), z)
    above = (kpt(x, up, core), z)
    below = (kpt(x, down, core), z)
    ahead = (me, lax.rem(z + 1, VIR))
    behind = (me, lax.rem(z + VIR - 1, VIR))

    def place(xx, yy, cc):
        return ((xx % 2) * 4 + yy) * 2 + cc

    spot_me = place(x, y, core)

    barrier = pltpu.get_barrier_semaphore()
    loop(1, KPT, lambda i: signal(barrier, (lax.rem(me + i, KPT), z)))
    signal(barrier, ahead)
    signal(barrier, behind)
    loads = [
        pltpu.make_async_copy(src, dst, load_sem.at[number])
        for number, (src, dst) in enumerate(
            ((df_ref.at[pl.ds(2, 2)], raw), (amp_hbm, amp_ref), (rest_hbm, rest_ref))
        )
    ]
    for load in loads:
        load.start()

    def pair_slot(slot):
        inverse = jnp.int32(0)
        for other in range(1, 4):
            inverse = jnp.where(slots_ref[other] == slot, jnp.int32(other), inverse)
        return jnp.where(half == 0, slots_ref[slot], inverse)

    by_half = one_hot(
        512, 512, lambda n: bits(n, 5, 1) * 256 + bits(n, 0, 5) * 8 + bits(n, 6, 3)
    )
    loads[0].wait()
    for side_half in range(2):
        picked = dot(raw[...].reshape(512, 512), by_half[:, side_half * 256 : side_half * 256 + 256])
        right[side_half] = picked.astype(BF16).reshape(HALF, 32, 256)

    pl.semaphore_wait(barrier, KPT + 1)

    def spread(kind, source, to):
        pair = to % HALF
        rows = pl.ds(pl.multiple_of((source // 4) * 32, 32), 32)
        slot = source % 4
        if kind == 0:
            return right.at[to // HALF, pair], far.at[slot, rows]
        return chunk.at[to], got.at[source]

    def spread_copy(kind, source, to):
        src, dst = spread(kind, source, to)
        return remote(src, dst, send_sem.at[kind, to], recv_sem.at[kind, source], (to, z))

    def own_spread(kind):
        src, dst = spread(kind, me, me)
        return pltpu.make_async_copy(src, dst, own_sem.at[kind])

    def spread_start(kind):
        loop(1, KPT, lambda i: spread_copy(kind, me, lax.rem(me + i, KPT)).start())
        own_spread(kind).start()

    def spread_recv(kind):
        loop(1, KPT, lambda i: spread_copy(kind, lax.rem(me + KPT - i, KPT), me).wait_recv())
        own_spread(kind).wait()

    def spread_sent(kind):
        loop(1, KPT, lambda i: spread_copy(kind, me, lax.rem(me + i, KPT)).wait_send())

    spread_start(0)

    line = y * 2 + core

    def slab_y(source, to):
        return remote(
            df_ref.at[pl.ds(0, 2), to], middle.at[:, source // 4, source % 4], slab_send.at[0, to], slab_recv.at[0, source],
            (x * 8 + to, z),
        )

    def slab_x(source, to):
        return remote(
            middle.at[to % 2], slab.at[pl.ds(2 * source, 2)], slab_send.at[1, to], slab_recv.at[1, source],
            (to * 8 + line, z),
        )

    own_y = pltpu.make_async_copy(df_ref.at[pl.ds(0, 2), line], middle.at[:, line // 4, line % 4], own_sem.at[2])
    own_x = pltpu.make_async_copy(middle.at[x % 2], slab.at[pl.ds(2 * x, 2)], own_sem.at[4])
    loop(1, 8, lambda i: slab_y(line, lax.rem(line + i, 8)).start())
    own_y.start()

    loads[1].wait()
    order = one_hot(
        128, 128, lambda n: bits(n, 6, 1) * 64 + bits(n, 0, 6)
    )
    lined = jnp.concatenate(
        [dot_rows(order, amp_ref[0, slot]).astype(BF16) for slot in range(4)], axis=0
    )
    to_owner = one_hot(
        512, 512,
        lambda n: bits(n, 2, 2) * 128 + bits(n, 0, 1) * 64 + bits(n, 4, 5) * 2 + bits(n, 1, 1),
    )
    chunk[...] = dot(to_owner, lined).astype(BF16).reshape(KPT, 16, 256)
    spread_start(1)

    turn = one_hot(256, 256, lambda n: bits(n, 0, 4) * 16 + bits(n, 4, 4))
    for slot in range(4):
        turned = dot(turn, amp_ref[1, slot]).astype(BF16)
        amps[spot_me, 4 + slot] = dot_rows(order, turned).astype(BF16)

    plan = (
        ((x, y), 0, 4, above), ((x, y), 0, 4, below), ((x, y), 0, 4, side),
        ((x_near, y), 0, 4, above), ((x_near, y), 0, 4, below),
        ((x, down), 0, 2, above), ((x, up), 2, 2, below), ((x, opposite), 0, 4, side),
    )
    arrive = (
        ((x, down), 0, 4), ((x, up), 0, 4), ((x_near, y), 0, 4),
        ((x_near, down), 0, 4), ((x_near, up), 0, 4),
        ((x, opposite), 0, 2), ((x, opposite), 2, 2), ((x_near, opposite), 0, 4),
        ((x, y), 0, 4),
    )

    def amp_copy(group, number):
        (xx, yy), low, count, device = plan[number]
        spot = amps.at[place(xx, yy, core), pl.ds(group * 4 + low, count)]
        return remote(spot, spot, amp_send.at[group, number], amp_recv.at[group, number], device)

    def amp_wait(group, number):
        (xx, yy), low, count = arrive[number]
        spot = amps.at[place(xx, yy, core), pl.ds(group * 4 + low, count)]
        remote(spot, spot, amp_send.at[group, number], amp_recv.at[group, number], mate).wait_recv()

    def mate_copy(group, number, whose):
        (xx, yy), low, count = arrive[number]
        spot = amps.at[place(xx, yy, whose), pl.ds(group * 4 + low, count)]
        return remote(spot, spot, mate_send.at[group, number], mate_recv.at[group, number], mate)

    def amp_begin(group):
        for number in range(3):
            amp_copy(group, number).start()
        mate_copy(group, 8, core).start()

    def amp_steps(group, numbers, forward):
        for number in numbers:
            amp_wait(group, number)
        for number in forward:
            amp_copy(group, number).start()
        for number in numbers:
            mate_copy(group, number, core).start()

    amp_begin(1)

    column = lax.broadcasted_iota(jnp.int32, (64, 64), 1)
    diagonal = lax.broadcasted_iota(jnp.int32, (64, 64), 0) == column
    spread_vir = jnp.where(diagonal, jnp.broadcast_to(vir_ref[...].astype(F32), (64, 64)), 0.0)
    senergy[...] = dot(spread_vir.astype(BF16), jnp.ones((64, 128), BF16))
    energy_copy = remote(
        senergy, menergy, rest_send.at[VIR], rest_recv.at[VIR], (mirror, z)
    )
    energy_copy.start()

    spread_recv(0)
    eye = one_hot(256, 256, lambda n: n)
    for slot in range(4):
        turned = dot_rows(eye, far[pair_slot(slot)]).astype(BF16)
        tiles[z, slot] = jnp.where(slot < live_ref[0], turned, jnp.zeros_like(turned))

    def ring(way, hop, slot):
        held = lax.rem(z + (VIR - hop if way == 0 else hop), VIR)
        spot = tiles.at[held, slot]
        return remote(
            spot, spot, ring_send.at[way, hop, slot], ring_recv.at[way, hop, slot],
            ahead if way == 0 else behind,
        )

    def ring_wait(way, hop, slot):
        held = lax.rem(z + (VIR - hop - 1 if way == 0 else hop + 1), VIR)
        spot = tiles.at[held, slot]
        remote(
            spot, spot, ring_send.at[way, hop, slot], ring_recv.at[way, hop, slot],
            ahead if way == 0 else behind,
        ).wait_recv()

    def ways(hop, slot):
        if hop < 3:
            return (0, 1)
        return (0,) if slot < 2 else (1,)

    for slot in range(4):
        for way in (0, 1):
            ring(way, 0, slot).start()

    def ring_step(hop, slot):
        for way in ways(hop, slot):
            ring_wait(way, hop, slot)
        if hop < 3:
            for way in ways(hop + 1, slot):
                ring(way, hop + 1, slot).start()

    low = lax.broadcasted_iota(jnp.int32, (8, 8, 128), 2) < 64

    def couple(tile, slot):
        product = dot(tiles[tile, slot], slab[:, slot].reshape(256, 512)).reshape(8, 4, 8, 512)
        for pair in range(4):
            piece = product[..., pair * 128 : (pair + 1) * 128]
            evens, odds = [], []
            for first in (0, 2):
                here, there = piece[:, first], piece[:, first + 1]
                evens.append(jnp.where(low, here, pltpu.roll(there, 64, 2)))
                odds.append(jnp.where(low, pltpu.roll(here, 64, 2), there))
            block = jnp.concatenate(
                [jnp.concatenate(evens, axis=2), jnp.concatenate(odds, axis=2)], axis=1
            )
            block = block.astype(BF16)
            for run in range(8):
                coupled[slot, tile, pair * 16 : pair * 16 + 16, run * 256 : run * 256 + 256] = block[run]

    def couple_two(hop, slot):
        loop(0, 2, lambda i: couple(lax.rem(z + VIR + (2 * i - 1) * (hop + 1), VIR), slot))

    loop(1, 8, lambda i: slab_y(lax.rem(line + 8 - i, 8), line).wait_recv())
    own_y.wait()
    loop(1, 4, lambda i: slab_x(x, lax.rem(x + i, 4)).start())
    own_x.start()

    spread_recv(1)
    regroup = one_hot(
        512, 512,
        lambda n: bits(n, 1, 5) * 16 + bits(n, 7, 2) * 4 + bits(n, 6, 1) * 2 + bits(n, 0, 1),
    )
    regrouped = dot(regroup, got[...].reshape(512, 256)).astype(BF16)
    amps[spot_me, 0:4] = regrouped.reshape(4, 128, 256)
    amp_begin(0)

    mover[...] = one_hot(512, 512, lambda n: bits(n, 0, 6) * 8 + bits(n, 6, 3))
    turner[...] = turn
    loads[2].wait()

    def rest_copy(source, to):
        return remote(
            srest.at[to], mrest.at[source], rest_send.at[to], rest_recv.at[source], (mirror, to)
        )

    @pl.when(half == 1)
    def _():
        rest = rest_ref[...].astype(F32)
        for tile in range(VIR):
            srest[tile] = rest[:, tile * 8 : tile * 8 + 8, :].reshape(64, 256).astype(BF16)

    for slot in range(4):
        ring_step(0, slot)
    amp_steps(1, (2, 0, 1), (3, 4, 5, 6))
    ring_step(1, 0)
    amp_steps(0, (2, 0, 1), (3, 4, 5, 6))
    ring_step(1, 1)
    loop(1, 4, lambda i: slab_x(lax.rem(x + 4 - i, 4), x).wait_recv())
    own_x.wait()
    loop(0, 4, lambda slot: couple(z, slot))
    ring_step(1, 2)
    for slot in (0, 1):
        couple_two(0, slot)
    ring_step(1, 3)
    for slot in (2, 3):
        couple_two(0, slot)
    amp_steps(1, (5, 6), (7,))
    ring_step(2, 0)
    amp_steps(0, (5, 6), (7,))
    ring_step(2, 1)
    for slot in (0, 1):
        couple_two(1, slot)
    amp_steps(1, (3, 4), ())
    ring_step(2, 2)
    couple_two(1, 2)
    ring_step(2, 3)
    couple_two(1, 3)
    amp_steps(0, (3, 4), ())
    for slot in range(4):
        ring_step(3, slot)
        couple_two(2, slot)

    @pl.when(half == 1)
    def _():
        loop(0, VIR, lambda i: rest_copy(z, lax.rem(z + i, VIR)).start())

    loop(0, 4, lambda slot: couple(lax.rem(z + 4, VIR), slot))
    amp_steps(1, (7,), ())
    amp_steps(0, (7,), ())
    for group in range(2):
        for number in range(9):
            mate_copy(group, number, 1 - core).wait_recv()

    for slot in range(4):
        both = amps[:, slot] + amps[:, 4 + pair_slot(slot)]
        summed_amps[slot] = both.reshape(2048, 256)

    def piece_copy(kind, source, to, device):
        return remote(
            part.at[to], shared.at[kind, source], swap_send.at[kind, to], swap_recv.at[kind, source],
            (device, to),
        )

    def pair_copy(pair):
        two = pl.ds(2 * pair, 2)
        return remote(
            part.at[two], shared.at[0, two], swap_send.at[2, pair], swap_recv.at[2, pair], (mirror, z)
        )

    own_piece = pltpu.make_async_copy(part.at[z], shared.at[1, z], own_sem.at[3])

    def ladder(step):
        pair = lax.rem(z // 2 + 2 + step, 4)
        two = pl.ds(2 * pair, 2)
        partial = dot(coupled[0, two].reshape(128, 2048), summed_amps[0])
        for slot in range(1, 4):
            partial = partial + dot(coupled[slot, two].reshape(128, 2048), summed_amps[slot])
        total[two] = partial.reshape(2, 64, 256)

        @pl.when(half == 0)
        def _():
            rest = rest_ref[:, pl.ds(pl.multiple_of(pair * 16, 16), 16), :].astype(F32)
            for one in range(2):
                total[2 * pair + one] += rest[:, one * 8 : one * 8 + 8, :].reshape(64, 256)

        part[two] = total[two].astype(BF16)

        @pl.when(half == 0)
        def _():
            for one in range(2):
                piece_copy(0, z, 2 * pair + one, mirror).start()

        @pl.when(half == 1)
        def _():
            pair_copy(pair).start()
            for one in range(2):
                to = 2 * pair + one

                @pl.when(to != z)
                def _():
                    piece_copy(1, z, to, me).start()

                @pl.when(to == z)
                def _():
                    own_piece.start()

    loop(0, 4, ladder)

    row = lax.broadcasted_iota(jnp.int32, (16, 256), 0)
    lane = lax.broadcasted_iota(jnp.int32, (16, 256), 1)
    occ_values = occ_ref[...]
    occ_first = dot(occ_values, jnp.where(lane // 16 == row, 1.0, 0.0).astype(BF16))
    occ_second = dot(occ_values, jnp.where(lane % 16 == row, 1.0, 0.0).astype(BF16))
    occ = jnp.where(
        half == 0, occ_first[0:1] + occ_second[1:2], occ_first[1:2] + occ_second[0:1]
    )
    energy_copy.wait_recv()

    def finish(own, flipped):
        summed = 0.0
        for block in flipped:
            moved = dot(mover[...], block.reshape(512, 256)).astype(BF16)
            summed = summed + dot(moved, turner[...])
        summed = summed.reshape(8, 64, 256)
        distant = jnp.concatenate([menergy[...]] * 2, axis=1)
        for v in range(8):
            near = jnp.concatenate([senergy[pl.ds(z * 8 + v, 1), :]] * 2, axis=1)
            out_ref[v] = ((own(v) + summed[v]) / (occ - near - distant)).astype(BF16)

    @pl.when(half == 0)
    def _():
        loop(0, VIR, lambda i: rest_copy(lax.rem(z + i, VIR), z).wait_recv())
        for pair in range(4):
            pair_copy(pair).wait_recv()

        def own(v):
            rows = slice(v * 8, v * 8 + 8)
            return (total[:, rows, :] + shared[0, :, rows, :].astype(F32)).reshape(64, 256)

        finish(own, (mrest[...],))
        loop(0, VIR, lambda i: piece_copy(0, z, lax.rem(z + i, VIR), mirror).wait_send())

    @pl.when(half == 1)
    def _():
        loop(0, VIR, lambda i: piece_copy(0, lax.rem(z + i, VIR), z, me).wait_recv())
        loop(1, VIR, lambda i: piece_copy(1, lax.rem(z + i, VIR), z, me).wait_recv())
        own_piece.wait()
        finish(lambda v: rest_ref[v].astype(F32), (shared[0], shared[1]))
        loop(1, VIR, lambda i: piece_copy(1, z, lax.rem(z + i, VIR), me).wait_send())
        for pair in range(4):
            pair_copy(pair).wait_send()
        loop(0, VIR, lambda i: rest_copy(z, lax.rem(z + i, VIR)).wait_send())

    for kind in range(2):
        spread_sent(kind)
    loop(1, 8, lambda i: slab_y(line, lax.rem(line + i, 8)).wait_send())
    loop(1, 4, lambda i: slab_x(x, lax.rem(x + i, 4)).wait_send())
    energy_copy.wait_send()
    for slot in range(4):
        for hop in range(4):
            for way in ways(hop, slot):
                ring(way, hop, slot).wait_send()
    for group in range(2):
        for number in range(8):
            amp_copy(group, number).wait_send()
        for number in range(9):
            mate_copy(group, number, core).wait_send()


def fused(slots, live, df, amp, rest, occ, vir):
    vmem = pl.BlockSpec(memory_space=pltpu.VMEM)
    smem = pl.BlockSpec(memory_space=pltpu.SMEM)
    hbm = pl.BlockSpec(memory_space=pl.ANY)
    dma = pltpu.SemaphoreType.DMA
    held = pltpu.VMEM
    return pl.pallas_call(
        fused_kernel,
        out_shape=jax.ShapeDtypeStruct((8, 64, 256), BF16),
        in_specs=[smem, smem, hbm, hbm, hbm, vmem, vmem],
        out_specs=vmem,
        scratch_shapes=[
            held((2, 8, 32, 512), BF16),
            held((2, 4, 256, 128), BF16),
            held((8, 64, 256), BF16),
            held((2, HALF, 32, 256), BF16),
            held((KPT, 16, 256), BF16),
            held((4, 256, 256), BF16),
            held((2, 2, 4, 32, 512), BF16),
            held((8, 4, 32, 512), BF16),
            held((KPT, 16, 256), BF16),
            held((VIR, 64, 256), BF16),
            held((VIR, 64, 256), BF16),
            held((64, 128), F32),
            held((64, 128), F32),
            held((VIR, 4, 256, 256), BF16),
            held((HALF, 8, 128, 256), BF16),
            held((4, VIR, 64, 2048), BF16),
            held((4, 2048, 256), BF16),
            held((VIR, 64, 256), F32),
            held((VIR, 64, 256), BF16),
            held((2, VIR, 64, 256), BF16),
            held((512, 512), BF16),
            held((256, 256), BF16),
            dma((5,)),
            dma((3,)),
            dma((2, KPT)),
            dma((2, KPT)),
            dma((2, 8)),
            dma((2, 8)),
            dma((VIR + 1,)),
            dma((VIR + 1,)),
            dma((2, 4, 4)),
            dma((2, 4, 4)),
            dma((2, 8)),
            dma((2, 8)),
            dma((2, 9)),
            dma((2, 9)),
            dma((3, VIR)),
            dma((3, VIR)),
        ],
        compiler_params=pltpu.CompilerParams(
            collective_id=0, has_side_effects=True, vmem_limit_bytes=56 * 1024 * 1024
        ),
        name="fused",
    )(slots, live, df, amp, rest, occ, vir)


def shards(df_pieces, amplitudes, rest_residual, occ_energy, vir_energy, live_slots, mirror_slot):
    out = fused(
        mirror_slot[0], live_slots, df_pieces.reshape(4, 8, 32, 512), amplitudes, rest_residual[0],
        occ_energy, vir_energy,
    )
    return out[None]


def solution(mesh):
    placed = (
        P("kpt", None, None, "vir"),
        P(None, None, None, "kpt"),
        P("kpt", "vir", None, None),
        P(),
        P("kpt", None),
        P("kpt"),
        P("kpt", None),
    )
    return jax.shard_map(
        shards, mesh=mesh, in_specs=placed, out_specs=P("kpt", "vir", None, None), check_vma=False
    )
```

```python
import jax
import jax.numpy as jnp
from jax import lax
from jax.experimental import pallas as pl
from jax.experimental.pallas import tpu as pltpu
from jax.sharding import PartitionSpec as P

MESH = pl.DeviceIdType.MESH
BF16 = jnp.bfloat16
F32 = jnp.float32
KPT = 32
VIR = 8
HALF = 16


def remote(src, dst, send, recv, device):
    return pltpu.make_async_remote_copy(
        src_ref=src, dst_ref=dst, send_sem=send, recv_sem=recv, device_id=device, device_id_type=MESH
    )


def signal(sem, device):
    pl.semaphore_signal(sem, inc=1, device_id=device, device_id_type=MESH)


def loop(low, high, body):
    def step(index, carry):
        body(index)
        return carry

    lax.fori_loop(low, high, step, 0)


def one_hot(rows, columns, target):
    row = lax.broadcasted_iota(jnp.int32, (rows, columns), 0)
    column = lax.broadcasted_iota(jnp.int32, (rows, columns), 1)
    return jnp.where(target(row) == column, 1.0, 0.0).astype(BF16)


def dot(left, right):
    return jnp.dot(left, right, preferred_element_type=F32)


def dot_rows(left, right):
    return lax.dot_general(left, right, (((1,), (1,)), ((), ())), preferred_element_type=F32)


def bits(value, low, count):
    return (value >> low) & ((1 << count) - 1)


def fused_kernel(
    slots_ref, live_ref, df_ref, amp_hbm, rest_hbm, occ_ref, vir_ref, out_ref,
    raw, amp_ref, rest_ref, right, chunk, far, middle, slab, got, srest, mrest, senergy, menergy,
    tiles, amps, coupled, summed_amps, total, part, whole, restored, shared, mover, turner,
    own_sem, load_sem, send_sem, recv_sem, slab_send, slab_recv, rest_send, rest_recv,
    ring_send, ring_recv, amp_send, amp_recv, mate_send, mate_recv, swap_send, swap_recv,
):
    me = lax.axis_index("kpt")
    z = lax.axis_index("vir")
    half = me // HALF
    mirror = lax.rem(me + HALF, KPT)
    core = me % 2
    y = (me // 2) % 4
    x = me // 8
    x_near = x + 1 - 2 * (x % 2)

    def kpt(xx, yy, cc):
        return (xx * 4 + yy) * 2 + cc

    up, down, opposite = (y + 1) % 4, (y + 3) % 4, (y + 2) % 4
    mate = (kpt(x, y, 1 - core), z)
    side = (kpt(x_near, y, core), z)
    above = (kpt(x, up, core), z)
    below = (kpt(x, down, core), z)
    ahead = (me, lax.rem(z + 1, VIR))
    behind = (me, lax.rem(z + VIR - 1, VIR))

    def place(xx, yy, cc):
        return ((xx % 2) * 4 + yy) * 2 + cc

    spot_me = place(x, y, core)

    barrier = pltpu.get_barrier_semaphore()
    loop(1, KPT, lambda i: signal(barrier, (lax.rem(me + i, KPT), z)))
    loop(1, VIR, lambda i: signal(barrier, (me, lax.rem(z + i, VIR))))
    loads = [
        pltpu.make_async_copy(src, dst, load_sem.at[number])
        for number, (src, dst) in enumerate(
            ((df_ref.at[pl.ds(2, 2)], raw), (amp_hbm, amp_ref), (rest_hbm, rest_ref))
        )
    ]
    for load in loads:
        load.start()

    def pair_slot(slot):
        inverse = jnp.int32(0)
        for other in range(1, 4):
            inverse = jnp.where(slots_ref[other] == slot, jnp.int32(other), inverse)
        return jnp.where(half == 0, slots_ref[slot], inverse)

    by_half = one_hot(
        512, 512, lambda n: bits(n, 5, 1) * 256 + bits(n, 0, 5) * 8 + bits(n, 6, 3)
    )
    loads[0].wait()
    for side_half in range(2):
        picked = dot(raw[...].reshape(512, 512), by_half[:, side_half * 256 : side_half * 256 + 256])
        right[side_half] = picked.astype(BF16).reshape(HALF, 32, 256)

    pl.semaphore_wait(barrier, KPT - 1 + VIR - 1)

    def spread(kind, source, to):
        pair = to % HALF
        rows = pl.ds(pl.multiple_of((source // 4) * 32, 32), 32)
        slot = source % 4
        if kind == 0:
            return right.at[to // HALF, pair], far.at[slot, rows]
        return chunk.at[to], got.at[source]

    def spread_copy(kind, source, to):
        src, dst = spread(kind, source, to)
        return remote(src, dst, send_sem.at[kind, to], recv_sem.at[kind, source], (to, z))

    def own_spread(kind):
        src, dst = spread(kind, me, me)
        return pltpu.make_async_copy(src, dst, own_sem.at[kind])

    def spread_start(kind):
        loop(1, KPT, lambda i: spread_copy(kind, me, lax.rem(me + i, KPT)).start())
        own_spread(kind).start()

    def spread_recv(kind):
        loop(1, KPT, lambda i: spread_copy(kind, lax.rem(me + KPT - i, KPT), me).wait_recv())
        own_spread(kind).wait()

    def spread_sent(kind):
        loop(1, KPT, lambda i: spread_copy(kind, me, lax.rem(me + i, KPT)).wait_send())

    spread_start(0)

    def rest_copy(source, to):
        return remote(
            srest.at[to], mrest.at[source], rest_send.at[to], rest_recv.at[source], (me, to)
        )

    own_rest = pltpu.make_async_copy(srest.at[z], mrest.at[z], load_sem.at[3])
    loads[2].wait()

    @pl.when(half == 1)
    def _():
        rest = rest_ref[...].astype(F32)
        for tile in range(VIR):
            srest[tile] = rest[:, tile * 8 : tile * 8 + 8, :].reshape(64, 256).astype(BF16)
        loop(1, VIR, lambda i: rest_copy(z, lax.rem(z + i, VIR)).start())
        own_rest.start()

    line = y * 2 + core

    def slab_y(source, to):
        return remote(
            df_ref.at[pl.ds(0, 2), to], middle.at[:, source // 4, source % 4], slab_send.at[0, to], slab_recv.at[0, source],
            (x * 8 + to, z),
        )

    def slab_x(source, to):
        return remote(
            middle.at[to % 2], slab.at[pl.ds(2 * source, 2)], slab_send.at[1, to], slab_recv.at[1, source],
            (to * 8 + line, z),
        )

    own_y = pltpu.make_async_copy(df_ref.at[pl.ds(0, 2), line], middle.at[:, line // 4, line % 4], own_sem.at[2])
    own_x = pltpu.make_async_copy(middle.at[x % 2], slab.at[pl.ds(2 * x, 2)], own_sem.at[4])
    loop(1, 8, lambda i: slab_y(line, lax.rem(line + i, 8)).start())
    own_y.start()

    loads[1].wait()
    order = one_hot(
        128, 128, lambda n: bits(n, 6, 1) * 64 + bits(n, 0, 6)
    )
    lined = jnp.concatenate(
        [dot_rows(order, amp_ref[0, slot]).astype(BF16) for slot in range(4)], axis=0
    )
    to_owner = one_hot(
        512, 512,
        lambda n: bits(n, 2, 2) * 128 + bits(n, 0, 1) * 64 + bits(n, 4, 5) * 2 + bits(n, 1, 1),
    )
    chunk[...] = dot(to_owner, lined).astype(BF16).reshape(KPT, 16, 256)
    spread_start(1)

    turn = one_hot(256, 256, lambda n: bits(n, 0, 4) * 16 + bits(n, 4, 4))
    for slot in range(4):
        turned = dot(turn, amp_ref[1, slot]).astype(BF16)
        amps[spot_me, 4 + slot] = dot_rows(order, turned).astype(BF16)

    plan = (
        ((x, y), 0, 4, above), ((x, y), 0, 4, below), ((x, y), 0, 4, side),
        ((x_near, y), 0, 4, above), ((x_near, y), 0, 4, below),
        ((x, down), 0, 2, above), ((x, up), 2, 2, below), ((x, opposite), 0, 4, side),
    )
    arrive = (
        ((x, down), 0, 4), ((x, up), 0, 4), ((x_near, y), 0, 4),
        ((x_near, down), 0, 4), ((x_near, up), 0, 4),
        ((x, opposite), 0, 2), ((x, opposite), 2, 2), ((x_near, opposite), 0, 4),
        ((x, y), 0, 4),
    )

    def amp_copy(group, number):
        (xx, yy), low, count, device = plan[number]
        spot = amps.at[place(xx, yy, core), pl.ds(group * 4 + low, count)]
        return remote(spot, spot, amp_send.at[group, number], amp_recv.at[group, number], device)

    def amp_wait(group, number):
        (xx, yy), low, count = arrive[number]
        spot = amps.at[place(xx, yy, core), pl.ds(group * 4 + low, count)]
        remote(spot, spot, amp_send.at[group, number], amp_recv.at[group, number], mate).wait_recv()

    def mate_copy(group, number, whose):
        (xx, yy), low, count = arrive[number]
        spot = amps.at[place(xx, yy, whose), pl.ds(group * 4 + low, count)]
        return remote(spot, spot, mate_send.at[group, number], mate_recv.at[group, number], mate)

    def amp_begin(group):
        for number in range(3):
            amp_copy(group, number).start()
        mate_copy(group, 8, core).start()

    def amp_steps(group, numbers, forward):
        for number in numbers:
            amp_wait(group, number)
        for number in forward:
            amp_copy(group, number).start()
        for number in numbers:
            mate_copy(group, number, core).start()

    amp_begin(1)

    column = lax.broadcasted_iota(jnp.int32, (64, 64), 1)
    diagonal = lax.broadcasted_iota(jnp.int32, (64, 64), 0) == column
    spread_vir = jnp.where(diagonal, jnp.broadcast_to(vir_ref[...].astype(F32), (64, 64)), 0.0)
    senergy[...] = dot(spread_vir.astype(BF16), jnp.ones((64, 128), BF16))
    energy_copy = remote(
        senergy, menergy, rest_send.at[VIR], rest_recv.at[VIR], (mirror, z)
    )
    energy_copy.start()

    spread_recv(0)
    eye = one_hot(256, 256, lambda n: n)
    for slot in range(4):
        turned = dot_rows(eye, far[pair_slot(slot)]).astype(BF16)
        tiles[z, slot] = jnp.where(slot < live_ref[0], turned, jnp.zeros_like(turned))

    def ring(way, hop, slot):
        held = lax.rem(z + (VIR - hop if way == 0 else hop), VIR)
        spot = tiles.at[held, slot]
        return remote(
            spot, spot, ring_send.at[way, hop, slot], ring_recv.at[way, hop, slot],
            ahead if way == 0 else behind,
        )

    def ring_wait(way, hop, slot):
        held = lax.rem(z + (VIR - hop - 1 if way == 0 else hop + 1), VIR)
        spot = tiles.at[held, slot]
        remote(
            spot, spot, ring_send.at[way, hop, slot], ring_recv.at[way, hop, slot],
            ahead if way == 0 else behind,
        ).wait_recv()

    def ways(hop, slot):
        if hop < 3:
            return (0, 1)
        return (0,) if slot < 2 else (1,)

    for slot in range(4):
        for way in (0, 1):
            ring(way, 0, slot).start()

    def ring_step(hop, slot):
        for way in ways(hop, slot):
            ring_wait(way, hop, slot)
        if hop < 3:
            for way in ways(hop + 1, slot):
                ring(way, hop + 1, slot).start()

    low = lax.broadcasted_iota(jnp.int32, (8, 8, 128), 2) < 64

    def couple(tile, slot):
        product = dot(tiles[tile, slot], slab[:, slot].reshape(256, 512)).reshape(8, 4, 8, 512)
        for pair in range(4):
            piece = product[..., pair * 128 : (pair + 1) * 128]
            evens, odds = [], []
            for first in (0, 2):
                here, there = piece[:, first], piece[:, first + 1]
                evens.append(jnp.where(low, here, pltpu.roll(there, 64, 2)))
                odds.append(jnp.where(low, pltpu.roll(here, 64, 2), there))
            block = jnp.concatenate(
                [jnp.concatenate(evens, axis=2), jnp.concatenate(odds, axis=2)], axis=1
            )
            block = block.astype(BF16)
            for run in range(8):
                coupled[slot, tile, pair * 16 : pair * 16 + 16, run * 256 : run * 256 + 256] = block[run]

    def couple_two(hop, slot):
        loop(0, 2, lambda i: couple(lax.rem(z + VIR + (2 * i - 1) * (hop + 1), VIR), slot))

    loop(1, 8, lambda i: slab_y(lax.rem(line + 8 - i, 8), line).wait_recv())
    own_y.wait()
    loop(1, 4, lambda i: slab_x(x, lax.rem(x + i, 4)).start())
    own_x.start()

    spread_recv(1)
    regroup = one_hot(
        512, 512,
        lambda n: bits(n, 1, 5) * 16 + bits(n, 7, 2) * 4 + bits(n, 6, 1) * 2 + bits(n, 0, 1),
    )
    regrouped = dot(regroup, got[...].reshape(512, 256)).astype(BF16)
    amps[spot_me, 0:4] = regrouped.reshape(4, 128, 256)
    amp_begin(0)

    mover[...] = one_hot(512, 512, lambda n: bits(n, 0, 6) * 8 + bits(n, 6, 3))
    turner[...] = turn

    @pl.when(half == 1)
    def _():
        loop(1, VIR, lambda i: rest_copy(lax.rem(z + i, VIR), z).wait_recv())
        own_rest.wait()
        swapped = one_hot(
            512, 512, lambda n: bits(n, 6, 3) * 64 + bits(n, 0, 3) * 8 + bits(n, 3, 3)
        )
        moved = dot(swapped, mrest[...].reshape(512, 256)).astype(BF16)
        restored[...] = dot(moved, turner[...]).astype(BF16).reshape(VIR, 64, 256)

    ring_step(0, 0)
    ring_step(0, 1)
    ring_step(0, 2)
    ring_step(0, 3)
    amp_steps(1, (0, 1), (5, 6))
    amp_steps(1, (2,), (3, 4))
    ring_step(1, 0)
    amp_steps(0, (0, 1), (5, 6))
    amp_steps(0, (2,), (3, 4))
    ring_step(1, 1)
    ring_step(1, 2)
    ring_step(1, 3)
    amp_steps(1, (5, 6), (7,))
    ring_step(2, 0)
    loop(1, 4, lambda i: slab_x(lax.rem(x + 4 - i, 4), x).wait_recv())
    own_x.wait()
    loop(0, 4, lambda slot: couple(z, slot))
    couple_two(0, 0)
    couple_two(0, 1)
    ring_step(2, 1)
    amp_steps(0, (5, 6), (7,))
    couple_two(0, 2)
    couple_two(0, 3)
    ring_step(2, 2)
    couple_two(1, 0)
    couple_two(1, 1)
    ring_step(2, 3)
    couple_two(1, 2)
    couple_two(1, 3)
    amp_steps(1, (3, 4), ())
    amp_steps(0, (3, 4), ())
    couple_two(2, 0)
    couple_two(2, 1)
    ring_step(3, 0)
    ring_step(3, 2)
    couple_two(2, 2)
    couple(lax.rem(z + 4, VIR), 0)
    couple(lax.rem(z + 4, VIR), 2)
    couple_two(2, 3)
    ring_step(3, 1)
    ring_step(3, 3)
    couple(lax.rem(z + 4, VIR), 1)
    couple(lax.rem(z + 4, VIR), 3)
    amp_steps(1, (7,), ())
    amp_steps(0, (7,), ())
    for group in range(2):
        for number in range(9):
            mate_copy(group, number, 1 - core).wait_recv()

    for slot in range(4):
        both = amps[:, slot] + amps[:, 4 + pair_slot(slot)]
        summed_amps[slot] = both.reshape(2048, 256)

    def piece_copy(kind, source, to, device):
        return remote(
            part.at[to], shared.at[kind, source], swap_send.at[kind, to], swap_recv.at[kind, source],
            (device, to),
        )

    def pair_copy(pair):
        two = pl.ds(2 * pair, 2)
        return remote(
            whole.at[two], shared.at[0, two], swap_send.at[2, pair], swap_recv.at[2, pair], (mirror, z)
        )

    own_piece = pltpu.make_async_copy(part.at[z], shared.at[1, z], own_sem.at[3])

    def ladder(step):
        pair = lax.rem(z // 2 + 2 + step, 4)
        two = pl.ds(2 * pair, 2)
        partial = dot(coupled[0, two].reshape(128, 2048), summed_amps[0])
        for slot in range(1, 4):
            partial = partial + dot(coupled[slot, two].reshape(128, 2048), summed_amps[slot])
        total[two] = partial.reshape(2, 64, 256)

        @pl.when(half == 0)
        def _():
            rest = rest_ref[:, pl.ds(pl.multiple_of(pair * 16, 16), 16), :].astype(F32)
            for one in range(2):
                total[2 * pair + one] += rest[:, one * 8 : one * 8 + 8, :].reshape(64, 256)

        part[two] = total[two].astype(BF16)

        @pl.when(half == 0)
        def _():
            for one in range(2):
                piece_copy(0, z, 2 * pair + one, mirror).start()

        @pl.when(half == 1)
        def _():
            whole[two] = (total[two] + restored[two].astype(F32)).astype(BF16)
            pair_copy(pair).start()
            for one in range(2):
                to = 2 * pair + one

                @pl.when(to != z)
                def _():
                    piece_copy(1, z, to, me).start()

                @pl.when(to == z)
                def _():
                    own_piece.start()

    loop(0, 4, ladder)

    row = lax.broadcasted_iota(jnp.int32, (16, 256), 0)
    lane = lax.broadcasted_iota(jnp.int32, (16, 256), 1)
    occ_values = occ_ref[...]
    occ_first = dot(occ_values, jnp.where(lane // 16 == row, 1.0, 0.0).astype(BF16))
    occ_second = dot(occ_values, jnp.where(lane % 16 == row, 1.0, 0.0).astype(BF16))
    occ = jnp.where(
        half == 0, occ_first[0:1] + occ_second[1:2], occ_first[1:2] + occ_second[0:1]
    )
    energy_copy.wait_recv()

    def finish(own, flipped):
        summed = 0.0
        for block in flipped:
            moved = dot(mover[...], block.reshape(512, 256)).astype(BF16)
            summed = summed + dot(moved, turner[...])
        summed = summed.reshape(8, 64, 256) if flipped else None
        distant = jnp.concatenate([menergy[...]] * 2, axis=1)
        for v in range(8):
            near = jnp.concatenate([senergy[pl.ds(z * 8 + v, 1), :]] * 2, axis=1)
            out_ref[v] = ((own(v) if summed is None else own(v) + summed[v]) / (occ - near - distant)).astype(BF16)

    @pl.when(half == 0)
    def _():
        for pair in range(4):
            pair_copy(pair).wait_recv()

        def own(v):
            rows = slice(v * 8, v * 8 + 8)
            return (total[:, rows, :] + shared[0, :, rows, :].astype(F32)).reshape(64, 256)

        finish(own, ())
        loop(0, VIR, lambda i: piece_copy(0, z, lax.rem(z + i, VIR), mirror).wait_send())

    @pl.when(half == 1)
    def _():
        loop(0, VIR, lambda i: piece_copy(0, lax.rem(z + i, VIR), z, me).wait_recv())
        loop(1, VIR, lambda i: piece_copy(1, lax.rem(z + i, VIR), z, me).wait_recv())
        own_piece.wait()
        finish(lambda v: rest_ref[v].astype(F32), (shared[0], shared[1]))
        loop(1, VIR, lambda i: piece_copy(1, z, lax.rem(z + i, VIR), me).wait_send())
        for pair in range(4):
            pair_copy(pair).wait_send()
        loop(1, VIR, lambda i: rest_copy(z, lax.rem(z + i, VIR)).wait_send())

    for kind in range(2):
        spread_sent(kind)
    loop(1, 8, lambda i: slab_y(line, lax.rem(line + i, 8)).wait_send())
    loop(1, 4, lambda i: slab_x(x, lax.rem(x + i, 4)).wait_send())
    energy_copy.wait_send()
    for slot in range(4):
        for hop in range(4):
            for way in ways(hop, slot):
                ring(way, hop, slot).wait_send()
    for group in range(2):
        for number in range(8):
            amp_copy(group, number).wait_send()
        for number in range(9):
            mate_copy(group, number, core).wait_send()


def fused(slots, live, df, amp, rest, occ, vir):
    vmem = pl.BlockSpec(memory_space=pltpu.VMEM)
    smem = pl.BlockSpec(memory_space=pltpu.SMEM)
    hbm = pl.BlockSpec(memory_space=pl.ANY)
    dma = pltpu.SemaphoreType.DMA
    held = pltpu.VMEM
    return pl.pallas_call(
        fused_kernel,
        out_shape=jax.ShapeDtypeStruct((8, 64, 256), BF16),
        in_specs=[smem, smem, hbm, hbm, hbm, vmem, vmem],
        out_specs=vmem,
        scratch_shapes=[
            held((2, 8, 32, 512), BF16),
            held((2, 4, 256, 128), BF16),
            held((8, 64, 256), BF16),
            held((2, HALF, 32, 256), BF16),
            held((KPT, 16, 256), BF16),
            held((4, 256, 256), BF16),
            held((2, 2, 4, 32, 512), BF16),
            held((8, 4, 32, 512), BF16),
            held((KPT, 16, 256), BF16),
            held((VIR, 64, 256), BF16),
            held((VIR, 64, 256), BF16),
            held((64, 128), F32),
            held((64, 128), F32),
            held((VIR, 4, 256, 256), BF16),
            held((HALF, 8, 128, 256), BF16),
            held((4, VIR, 64, 2048), BF16),
            held((4, 2048, 256), BF16),
            held((VIR, 64, 256), F32),
            held((VIR, 64, 256), BF16),
            held((VIR, 64, 256), BF16),
            held((VIR, 64, 256), BF16),
            held((2, VIR, 64, 256), BF16),
            held((512, 512), BF16),
            held((256, 256), BF16),
            dma((5,)),
            dma((4,)),
            dma((2, KPT)),
            dma((2, KPT)),
            dma((2, 8)),
            dma((2, 8)),
            dma((VIR + 1,)),
            dma((VIR + 1,)),
            dma((2, 4, 4)),
            dma((2, 4, 4)),
            dma((2, 8)),
            dma((2, 8)),
            dma((2, 9)),
            dma((2, 9)),
            dma((3, VIR)),
            dma((3, VIR)),
        ],
        compiler_params=pltpu.CompilerParams(
            collective_id=0, has_side_effects=True, vmem_limit_bytes=56 * 1024 * 1024
        ),
        name="fused",
    )(slots, live, df, amp, rest, occ, vir)


def shards(df_pieces, amplitudes, rest_residual, occ_energy, vir_energy, live_slots, mirror_slot):
    out = fused(
        mirror_slot[0], live_slots, df_pieces.reshape(4, 8, 32, 512), amplitudes, rest_residual[0],
        occ_energy, vir_energy,
    )
    return out[None]


def solution(mesh):
    placed = (
        P("kpt", None, None, "vir"),
        P(None, None, None, "kpt"),
        P("kpt", "vir", None, None),
        P(),
        P("kpt", None),
        P("kpt"),
        P("kpt", None),
    )
    return jax.shard_map(
        shards, mesh=mesh, in_specs=placed, out_specs=P("kpt", "vir", None, None), check_vma=False
    )
```

```python
import jax
import jax.numpy as jnp
from jax import lax
from jax.experimental import pallas as pl
from jax.experimental.pallas import tpu as pltpu
from jax.sharding import PartitionSpec as P

MESH = pl.DeviceIdType.MESH
BF16 = jnp.bfloat16
F32 = jnp.float32
KPT = 32
VIR = 8
HALF = 16


def remote(src, dst, send, recv, device):
    return pltpu.make_async_remote_copy(
        src_ref=src, dst_ref=dst, send_sem=send, recv_sem=recv, device_id=device, device_id_type=MESH
    )


def signal(sem, device):
    pl.semaphore_signal(sem, inc=1, device_id=device, device_id_type=MESH)


def loop(low, high, body):
    def step(index, carry):
        body(index)
        return carry

    lax.fori_loop(low, high, step, 0)


def one_hot(rows, columns, target):
    row = lax.broadcasted_iota(jnp.int32, (rows, columns), 0)
    column = lax.broadcasted_iota(jnp.int32, (rows, columns), 1)
    return jnp.where(target(row) == column, 1.0, 0.0).astype(BF16)


def dot(left, right):
    return jnp.dot(left, right, preferred_element_type=F32)


def dot_rows(left, right):
    return lax.dot_general(left, right, (((1,), (1,)), ((), ())), preferred_element_type=F32)


def bits(value, low, count):
    return (value >> low) & ((1 << count) - 1)


def fused_kernel(
    slots_ref, live_ref, df_ref, amp_hbm, rest_hbm, occ_ref, vir_ref, out_ref,
    raw, amp_ref, rest_ref, right, chunk, far, middle, slab, got, srest, mrest, senergy, menergy,
    tiles, amps, coupled, summed_amps, total, part, whole, restored, shared, mover, turner,
    own_sem, load_sem, send_sem, recv_sem, slab_send, slab_recv, rest_send, rest_recv,
    ring_send, ring_recv, amp_send, amp_recv, mate_send, mate_recv, swap_send, swap_recv,
):
    me = lax.axis_index("kpt")
    z = lax.axis_index("vir")
    half = me // HALF
    mirror = lax.rem(me + HALF, KPT)
    core = me % 2
    y = (me // 2) % 4
    x = me // 8
    x_near = x + 1 - 2 * (x % 2)

    def kpt(xx, yy, cc):
        return (xx * 4 + yy) * 2 + cc

    up, down, opposite = (y + 1) % 4, (y + 3) % 4, (y + 2) % 4
    mate = (kpt(x, y, 1 - core), z)
    side = (kpt(x_near, y, core), z)
    above = (kpt(x, up, core), z)
    below = (kpt(x, down, core), z)
    ahead = (me, lax.rem(z + 1, VIR))
    behind = (me, lax.rem(z + VIR - 1, VIR))

    def place(xx, yy, cc):
        return ((xx % 2) * 4 + yy) * 2 + cc

    spot_me = place(x, y, core)

    barrier = pltpu.get_barrier_semaphore()
    loop(1, KPT, lambda i: signal(barrier, (lax.rem(me + i, KPT), z)))
    loop(1, VIR, lambda i: signal(barrier, (me, lax.rem(z + i, VIR))))
    loads = [
        pltpu.make_async_copy(src, dst, load_sem.at[number])
        for number, (src, dst) in enumerate(
            ((df_ref.at[pl.ds(2, 2)], raw), (amp_hbm, amp_ref), (rest_hbm, rest_ref))
        )
    ]
    for load in loads:
        load.start()

    def pair_slot(slot):
        inverse = jnp.int32(0)
        for other in range(1, 4):
            inverse = jnp.where(slots_ref[other] == slot, jnp.int32(other), inverse)
        return jnp.where(half == 0, slots_ref[slot], inverse)

    by_half = one_hot(
        512, 512, lambda n: bits(n, 5, 1) * 256 + bits(n, 0, 5) * 8 + bits(n, 6, 3)
    )
    loads[0].wait()
    for side_half in range(2):
        picked = dot(raw[...].reshape(512, 512), by_half[:, side_half * 256 : side_half * 256 + 256])
        right[side_half] = picked.astype(BF16).reshape(HALF, 32, 256)

    pl.semaphore_wait(barrier, KPT - 1 + VIR - 1)

    def spread(kind, source, to):
        pair = to % HALF
        rows = pl.ds(pl.multiple_of((source // 4) * 32, 32), 32)
        slot = source % 4
        if kind == 0:
            return right.at[to // HALF, pair], far.at[slot, rows]
        return chunk.at[to], got.at[source]

    def spread_copy(kind, source, to):
        src, dst = spread(kind, source, to)
        return remote(src, dst, send_sem.at[kind, to], recv_sem.at[kind, source], (to, z))

    def own_spread(kind):
        src, dst = spread(kind, me, me)
        return pltpu.make_async_copy(src, dst, own_sem.at[kind])

    def spread_start(kind):
        loop(1, KPT, lambda i: spread_copy(kind, me, lax.rem(me + i, KPT)).start())
        own_spread(kind).start()

    def spread_recv(kind):
        loop(1, KPT, lambda i: spread_copy(kind, lax.rem(me + KPT - i, KPT), me).wait_recv())
        own_spread(kind).wait()

    def spread_sent(kind):
        loop(1, KPT, lambda i: spread_copy(kind, me, lax.rem(me + i, KPT)).wait_send())

    spread_start(0)

    line = y * 2 + core

    def slab_y(source, to):
        return remote(
            df_ref.at[pl.ds(0, 2), to], middle.at[:, source // 4, source % 4], slab_send.at[0, to], slab_recv.at[0, source],
            (x * 8 + to, z),
        )

    def slab_x(source, to):
        return remote(
            middle.at[to % 2], slab.at[pl.ds(2 * source, 2)], slab_send.at[1, to], slab_recv.at[1, source],
            (to * 8 + line, z),
        )

    own_y = pltpu.make_async_copy(df_ref.at[pl.ds(0, 2), line], middle.at[:, line // 4, line % 4], own_sem.at[2])
    own_x = pltpu.make_async_copy(middle.at[x % 2], slab.at[pl.ds(2 * x, 2)], own_sem.at[4])
    loop(1, 8, lambda i: slab_y(line, lax.rem(line + i, 8)).start())
    own_y.start()

    loads[1].wait()
    order = one_hot(
        128, 128, lambda n: bits(n, 6, 1) * 64 + bits(n, 0, 6)
    )
    lined = jnp.concatenate(
        [dot_rows(order, amp_ref[0, slot]).astype(BF16) for slot in range(4)], axis=0
    )
    to_owner = one_hot(
        512, 512,
        lambda n: bits(n, 2, 2) * 128 + bits(n, 0, 1) * 64 + bits(n, 4, 5) * 2 + bits(n, 1, 1),
    )
    chunk[...] = dot(to_owner, lined).astype(BF16).reshape(KPT, 16, 256)
    spread_start(1)

    def rest_copy(source, to):
        return remote(
            srest.at[to], mrest.at[source], rest_send.at[to], rest_recv.at[source], (me, to)
        )

    own_rest = pltpu.make_async_copy(srest.at[z], mrest.at[z], load_sem.at[3])
    loads[2].wait()

    @pl.when(half == 1)
    def _():
        rest = rest_ref[...].astype(F32)
        for tile in range(VIR):
            srest[tile] = rest[:, tile * 8 : tile * 8 + 8, :].reshape(64, 256).astype(BF16)
        loop(1, VIR, lambda i: rest_copy(z, lax.rem(z + i, VIR)).start())
        own_rest.start()

    turn = one_hot(256, 256, lambda n: bits(n, 0, 4) * 16 + bits(n, 4, 4))
    for slot in range(4):
        turned = dot(turn, amp_ref[1, slot]).astype(BF16)
        amps[spot_me, 4 + slot] = dot_rows(order, turned).astype(BF16)

    plan = (
        ((x, y), 0, 4, above), ((x, y), 0, 4, below), ((x, y), 0, 4, side),
        ((x_near, y), 0, 4, above), ((x_near, y), 0, 4, below),
        ((x, down), 0, 2, above), ((x, up), 2, 2, below), ((x, opposite), 0, 4, side),
    )
    arrive = (
        ((x, down), 0, 4), ((x, up), 0, 4), ((x_near, y), 0, 4),
        ((x_near, down), 0, 4), ((x_near, up), 0, 4),
        ((x, opposite), 0, 2), ((x, opposite), 2, 2), ((x_near, opposite), 0, 4),
        ((x, y), 0, 4),
    )

    def amp_copy(group, number):
        (xx, yy), low, count, device = plan[number]
        spot = amps.at[place(xx, yy, core), pl.ds(group * 4 + low, count)]
        return remote(spot, spot, amp_send.at[group, number], amp_recv.at[group, number], device)

    def amp_wait(group, number):
        (xx, yy), low, count = arrive[number]
        spot = amps.at[place(xx, yy, core), pl.ds(group * 4 + low, count)]
        remote(spot, spot, amp_send.at[group, number], amp_recv.at[group, number], mate).wait_recv()

    def mate_copy(group, number, whose):
        (xx, yy), low, count = arrive[number]
        spot = amps.at[place(xx, yy, whose), pl.ds(group * 4 + low, count)]
        return remote(spot, spot, mate_send.at[group, number], mate_recv.at[group, number], mate)

    def amp_begin(group):
        for number in (2, 0, 1):
            amp_copy(group, number).start()
        mate_copy(group, 8, core).start()

    def amp_steps(group, numbers, forward):
        for number in numbers:
            amp_wait(group, number)
        for number in forward:
            amp_copy(group, number).start()
        for number in numbers:
            mate_copy(group, number, core).start()

    amp_begin(1)

    column = lax.broadcasted_iota(jnp.int32, (64, 64), 1)
    diagonal = lax.broadcasted_iota(jnp.int32, (64, 64), 0) == column
    spread_vir = jnp.where(diagonal, jnp.broadcast_to(vir_ref[...].astype(F32), (64, 64)), 0.0)
    senergy[...] = dot(spread_vir.astype(BF16), jnp.ones((64, 128), BF16))
    energy_copy = remote(
        senergy, menergy, rest_send.at[VIR], rest_recv.at[VIR], (mirror, z)
    )
    energy_copy.start()

    spread_recv(0)
    eye = one_hot(256, 256, lambda n: n)
    for slot in range(4):
        turned = dot_rows(eye, far[pair_slot(slot)]).astype(BF16)
        tiles[z, slot] = jnp.where(slot < live_ref[0], turned, jnp.zeros_like(turned))

    def ring(way, hop, slot):
        held = lax.rem(z + (VIR - hop if way == 0 else hop), VIR)
        spot = tiles.at[held, slot]
        return remote(
            spot, spot, ring_send.at[way, hop, slot], ring_recv.at[way, hop, slot],
            ahead if way == 0 else behind,
        )

    def ring_wait(way, hop, slot):
        held = lax.rem(z + (VIR - hop - 1 if way == 0 else hop + 1), VIR)
        spot = tiles.at[held, slot]
        remote(
            spot, spot, ring_send.at[way, hop, slot], ring_recv.at[way, hop, slot],
            ahead if way == 0 else behind,
        ).wait_recv()

    def ways(hop, slot):
        if hop < 3:
            return (0, 1)
        return (0,) if slot < 2 else (1,)

    for slot in range(4):
        for way in (0, 1):
            ring(way, 0, slot).start()

    def ring_step(hop, slot):
        for way in ways(hop, slot):
            ring_wait(way, hop, slot)
        if hop < 3:
            for way in ways(hop + 1, slot):
                ring(way, hop + 1, slot).start()

    low = lax.broadcasted_iota(jnp.int32, (8, 8, 128), 2) < 64

    def couple(tile, slot):
        product = dot(tiles[tile, slot], slab[:, slot].reshape(256, 512)).reshape(8, 4, 8, 512)
        for pair in range(4):
            piece = product[..., pair * 128 : (pair + 1) * 128]
            evens, odds = [], []
            for first in (0, 2):
                here, there = piece[:, first], piece[:, first + 1]
                evens.append(jnp.where(low, here, pltpu.roll(there, 64, 2)))
                odds.append(jnp.where(low, pltpu.roll(here, 64, 2), there))
            block = jnp.concatenate(
                [jnp.concatenate(evens, axis=2), jnp.concatenate(odds, axis=2)], axis=1
            )
            block = block.astype(BF16)
            for run in range(8):
                coupled[slot, tile, pair * 16 : pair * 16 + 16, run * 256 : run * 256 + 256] = block[run]

    def couple_two(hop, slot):
        loop(0, 2, lambda i: couple(lax.rem(z + VIR + (2 * i - 1) * (hop + 1), VIR), slot))

    spread_recv(1)
    regroup = one_hot(
        512, 512,
        lambda n: bits(n, 1, 5) * 16 + bits(n, 7, 2) * 4 + bits(n, 6, 1) * 2 + bits(n, 0, 1),
    )
    regrouped = dot(regroup, got[...].reshape(512, 256)).astype(BF16)
    amps[spot_me, 0:4] = regrouped.reshape(4, 128, 256)
    amp_begin(0)

    loop(1, 8, lambda i: slab_y(lax.rem(line + 8 - i, 8), line).wait_recv())
    own_y.wait()
    for i in (2, 1, 3):
        slab_x(x, lax.rem(x + i, 4)).start()
    own_x.start()

    mover[...] = one_hot(512, 512, lambda n: bits(n, 0, 6) * 8 + bits(n, 6, 3))
    turner[...] = turn

    @pl.when(half == 1)
    def _():
        loop(1, VIR, lambda i: rest_copy(lax.rem(z + i, VIR), z).wait_recv())
        own_rest.wait()
        swapped = one_hot(
            512, 512, lambda n: bits(n, 6, 3) * 64 + bits(n, 0, 3) * 8 + bits(n, 3, 3)
        )
        moved = dot(swapped, mrest[...].reshape(512, 256)).astype(BF16)
        restored[...] = dot(moved, turner[...]).astype(BF16).reshape(VIR, 64, 256)

    ring_step(0, 0)
    ring_step(0, 1)
    ring_step(0, 2)
    ring_step(0, 3)
    amp_steps(1, (0, 1), (5, 6))
    amp_steps(1, (2,), (3, 4))
    ring_step(1, 0)
    amp_steps(0, (0, 1), (5, 6))
    amp_steps(0, (2,), (3, 4))
    ring_step(1, 1)
    ring_step(1, 2)
    ring_step(1, 3)
    amp_steps(1, (5, 6), (7,))
    ring_step(2, 0)
    loop(1, 4, lambda i: slab_x(lax.rem(x + 4 - i, 4), x).wait_recv())
    own_x.wait()
    loop(0, 4, lambda slot: couple(z, slot))
    couple_two(0, 0)
    couple_two(0, 1)
    ring_step(2, 1)
    amp_steps(0, (5, 6), (7,))
    couple_two(0, 2)
    couple_two(0, 3)
    ring_step(2, 2)
    couple_two(1, 0)
    couple_two(1, 1)
    ring_step(2, 3)
    couple_two(1, 2)
    couple_two(1, 3)
    amp_steps(1, (3, 4), ())
    amp_steps(0, (3, 4), ())
    couple_two(2, 0)
    couple_two(2, 1)
    ring_step(3, 0)
    ring_step(3, 2)
    couple_two(2, 2)
    couple(lax.rem(z + 4, VIR), 0)
    couple(lax.rem(z + 4, VIR), 2)
    couple_two(2, 3)
    ring_step(3, 1)
    ring_step(3, 3)
    couple(lax.rem(z + 4, VIR), 1)
    couple(lax.rem(z + 4, VIR), 3)
    amp_steps(1, (7,), ())
    amp_steps(0, (7,), ())
    for group in range(2):
        for number in range(9):
            mate_copy(group, number, 1 - core).wait_recv()

    for slot in range(4):
        both = amps[:, slot] + amps[:, 4 + pair_slot(slot)]
        summed_amps[slot] = both.reshape(2048, 256)

    def piece_copy(kind, source, to, device):
        return remote(
            part.at[to], shared.at[kind, source], swap_send.at[kind, to], swap_recv.at[kind, source],
            (device, to),
        )

    def pair_copy(pair):
        two = pl.ds(2 * pair, 2)
        return remote(
            whole.at[two], shared.at[0, two], swap_send.at[2, pair], swap_recv.at[2, pair], (mirror, z)
        )

    own_piece = pltpu.make_async_copy(part.at[z], shared.at[1, z], own_sem.at[3])

    def ladder(step):
        pair = lax.rem(z // 2 + jnp.where(step < 2, step + 2, 3 - step), 4)
        two = pl.ds(2 * pair, 2)
        partial = dot(coupled[0, two].reshape(128, 2048), summed_amps[0])
        for slot in range(1, 4):
            partial = partial + dot(coupled[slot, two].reshape(128, 2048), summed_amps[slot])
        total[two] = partial.reshape(2, 64, 256)

        @pl.when(half == 0)
        def _():
            rest = rest_ref[:, pl.ds(pl.multiple_of(pair * 16, 16), 16), :].astype(F32)
            for one in range(2):
                total[2 * pair + one] += rest[:, one * 8 : one * 8 + 8, :].reshape(64, 256)

        part[two] = total[two].astype(BF16)

        @pl.when(half == 0)
        def _():
            for one in range(2):
                piece_copy(0, z, 2 * pair + one, mirror).start()

        @pl.when(half == 1)
        def _():
            whole[two] = (total[two] + restored[two].astype(F32)).astype(BF16)
            pair_copy(pair).start()
            for one in range(2):
                to = 2 * pair + one

                @pl.when(to != z)
                def _():
                    piece_copy(1, z, to, me).start()

                @pl.when(to == z)
                def _():
                    own_piece.start()

    loop(0, 4, ladder)

    row = lax.broadcasted_iota(jnp.int32, (16, 256), 0)
    lane = lax.broadcasted_iota(jnp.int32, (16, 256), 1)
    occ_values = occ_ref[...]
    occ_first = dot(occ_values, jnp.where(lane // 16 == row, 1.0, 0.0).astype(BF16))
    occ_second = dot(occ_values, jnp.where(lane % 16 == row, 1.0, 0.0).astype(BF16))
    occ = jnp.where(
        half == 0, occ_first[0:1] + occ_second[1:2], occ_first[1:2] + occ_second[0:1]
    )
    energy_copy.wait_recv()

    def finish(own, flipped):
        summed = 0.0
        for block in flipped:
            moved = dot(mover[...], block.reshape(512, 256)).astype(BF16)
            summed = summed + dot(moved, turner[...])
        summed = summed.reshape(8, 64, 256) if flipped else None
        distant = jnp.concatenate([menergy[...]] * 2, axis=1)
        for v in range(8):
            near = jnp.concatenate([senergy[pl.ds(z * 8 + v, 1), :]] * 2, axis=1)
            out_ref[v] = ((own(v) if summed is None else own(v) + summed[v]) / (occ - near - distant)).astype(BF16)

    @pl.when(half == 0)
    def _():
        for pair in range(4):
            pair_copy(pair).wait_recv()

        def own(v):
            rows = slice(v * 8, v * 8 + 8)
            return (total[:, rows, :] + shared[0, :, rows, :].astype(F32)).reshape(64, 256)

        finish(own, ())
        loop(0, VIR, lambda i: piece_copy(0, z, lax.rem(z + i, VIR), mirror).wait_send())

    @pl.when(half == 1)
    def _():
        loop(0, VIR, lambda i: piece_copy(0, lax.rem(z + i, VIR), z, me).wait_recv())
        loop(1, VIR, lambda i: piece_copy(1, lax.rem(z + i, VIR), z, me).wait_recv())
        own_piece.wait()
        finish(lambda v: rest_ref[v].astype(F32), (shared[0], shared[1]))
        loop(1, VIR, lambda i: piece_copy(1, z, lax.rem(z + i, VIR), me).wait_send())
        for pair in range(4):
            pair_copy(pair).wait_send()
        loop(1, VIR, lambda i: rest_copy(z, lax.rem(z + i, VIR)).wait_send())

    for kind in range(2):
        spread_sent(kind)
    loop(1, 8, lambda i: slab_y(line, lax.rem(line + i, 8)).wait_send())
    loop(1, 4, lambda i: slab_x(x, lax.rem(x + i, 4)).wait_send())
    energy_copy.wait_send()
    for slot in range(4):
        for hop in range(4):
            for way in ways(hop, slot):
                ring(way, hop, slot).wait_send()
    for group in range(2):
        for number in range(8):
            amp_copy(group, number).wait_send()
        for number in range(9):
            mate_copy(group, number, core).wait_send()


def fused(slots, live, df, amp, rest, occ, vir):
    vmem = pl.BlockSpec(memory_space=pltpu.VMEM)
    smem = pl.BlockSpec(memory_space=pltpu.SMEM)
    hbm = pl.BlockSpec(memory_space=pl.ANY)
    dma = pltpu.SemaphoreType.DMA
    held = pltpu.VMEM
    return pl.pallas_call(
        fused_kernel,
        out_shape=jax.ShapeDtypeStruct((8, 64, 256), BF16),
        in_specs=[smem, smem, hbm, hbm, hbm, vmem, vmem],
        out_specs=vmem,
        scratch_shapes=[
            held((2, 8, 32, 512), BF16),
            held((2, 4, 256, 128), BF16),
            held((8, 64, 256), BF16),
            held((2, HALF, 32, 256), BF16),
            held((KPT, 16, 256), BF16),
            held((4, 256, 256), BF16),
            held((2, 2, 4, 32, 512), BF16),
            held((8, 4, 32, 512), BF16),
            held((KPT, 16, 256), BF16),
            held((VIR, 64, 256), BF16),
            held((VIR, 64, 256), BF16),
            held((64, 128), F32),
            held((64, 128), F32),
            held((VIR, 4, 256, 256), BF16),
            held((HALF, 8, 128, 256), BF16),
            held((4, VIR, 64, 2048), BF16),
            held((4, 2048, 256), BF16),
            held((VIR, 64, 256), F32),
            held((VIR, 64, 256), BF16),
            held((VIR, 64, 256), BF16),
            held((VIR, 64, 256), BF16),
            held((2, VIR, 64, 256), BF16),
            held((512, 512), BF16),
            held((256, 256), BF16),
            dma((5,)),
            dma((4,)),
            dma((2, KPT)),
            dma((2, KPT)),
            dma((2, 8)),
            dma((2, 8)),
            dma((VIR + 1,)),
            dma((VIR + 1,)),
            dma((2, 4, 4)),
            dma((2, 4, 4)),
            dma((2, 8)),
            dma((2, 8)),
            dma((2, 9)),
            dma((2, 9)),
            dma((3, VIR)),
            dma((3, VIR)),
        ],
        compiler_params=pltpu.CompilerParams(
            collective_id=0, has_side_effects=True, vmem_limit_bytes=56 * 1024 * 1024
        ),
        name="fused",
    )(slots, live, df, amp, rest, occ, vir)


def shards(df_pieces, amplitudes, rest_residual, occ_energy, vir_energy, live_slots, mirror_slot):
    out = fused(
        mirror_slot[0], live_slots, df_pieces.reshape(4, 8, 32, 512), amplitudes, rest_residual[0],
        occ_energy, vir_energy,
    )
    return out[None]


def solution(mesh):
    placed = (
        P("kpt", None, None, "vir"),
        P(None, None, None, "kpt"),
        P("kpt", "vir", None, None),
        P(),
        P("kpt", None),
        P("kpt"),
        P("kpt", None),
    )
    return jax.shard_map(
        shards, mesh=mesh, in_specs=placed, out_specs=P("kpt", "vir", None, None), check_vma=False
    )
```

```python
import jax
import jax.numpy as jnp
from jax import lax
from jax.experimental import pallas as pl
from jax.experimental.pallas import tpu as pltpu
from jax.sharding import PartitionSpec as P

MESH = pl.DeviceIdType.MESH
BF16 = jnp.bfloat16
F32 = jnp.float32
KPT = 32
VIR = 8
HALF = 16


def remote(src, dst, send, recv, device):
    return pltpu.make_async_remote_copy(
        src_ref=src, dst_ref=dst, send_sem=send, recv_sem=recv, device_id=device, device_id_type=MESH
    )


def signal(sem, device):
    pl.semaphore_signal(sem, inc=1, device_id=device, device_id_type=MESH)


def loop(low, high, body):
    def step(index, carry):
        body(index)
        return carry

    lax.fori_loop(low, high, step, 0)


def one_hot(rows, columns, target):
    row = lax.broadcasted_iota(jnp.int32, (rows, columns), 0)
    column = lax.broadcasted_iota(jnp.int32, (rows, columns), 1)
    return jnp.where(target(row) == column, 1.0, 0.0).astype(BF16)


def dot(left, right):
    return jnp.dot(left, right, preferred_element_type=F32)


def dot_rows(left, right):
    return lax.dot_general(left, right, (((1,), (1,)), ((), ())), preferred_element_type=F32)


def bits(value, low, count):
    return (value >> low) & ((1 << count) - 1)


def fused_kernel(
    slots_ref, live_ref, df_ref, amp_hbm, rest_hbm, occ_ref, vir_ref, out_ref,
    raw, amp_ref, rest_ref, right, chunk, far, middle, slab, got, srest, mrest, senergy, menergy,
    tiles, amps, coupled, summed_amps, total, part, whole, restored, shared, mover, turner,
    own_sem, load_sem, send_sem, recv_sem, slab_send, slab_recv, rest_send, rest_recv,
    ring_send, ring_recv, amp_send, amp_recv, mate_send, mate_recv, swap_send, swap_recv,
):
    me = lax.axis_index("kpt")
    z = lax.axis_index("vir")
    half = me // HALF
    mirror = lax.rem(me + HALF, KPT)
    core = me % 2
    y = (me // 2) % 4
    x = me // 8
    x_near = x + 1 - 2 * (x % 2)

    def kpt(xx, yy, cc):
        return (xx * 4 + yy) * 2 + cc

    up, down, opposite = (y + 1) % 4, (y + 3) % 4, (y + 2) % 4
    mate = (kpt(x, y, 1 - core), z)
    side = (kpt(x_near, y, core), z)
    above = (kpt(x, up, core), z)
    below = (kpt(x, down, core), z)
    ahead = (me, lax.rem(z + 1, VIR))
    behind = (me, lax.rem(z + VIR - 1, VIR))

    def place(xx, yy, cc):
        return ((xx % 2) * 4 + yy) * 2 + cc

    spot_me = place(x, y, core)

    barrier = pltpu.get_barrier_semaphore()
    loop(1, VIR, lambda i: signal(barrier, (me, lax.rem(z + i, VIR))))
    loop(0, KPT - 1, lambda i: signal(barrier, (lax.rem(me + lax.rem(i + 15, KPT - 1) + 1, KPT), z)))
    loads = [
        pltpu.make_async_copy(src, dst, load_sem.at[number])
        for number, (src, dst) in enumerate(
            ((df_ref.at[pl.ds(2, 2)], raw), (amp_hbm, amp_ref), (rest_hbm, rest_ref))
        )
    ]
    for load in loads:
        load.start()

    def pair_slot(slot):
        inverse = jnp.int32(0)
        for other in range(1, 4):
            inverse = jnp.where(slots_ref[other] == slot, jnp.int32(other), inverse)
        return jnp.where(half == 0, slots_ref[slot], inverse)

    by_half = one_hot(
        512, 512, lambda n: bits(n, 5, 1) * 256 + bits(n, 0, 5) * 8 + bits(n, 6, 3)
    )
    loads[0].wait()
    for side_half in range(2):
        picked = dot(raw[...].reshape(512, 512), by_half[:, side_half * 256 : side_half * 256 + 256])
        right[side_half] = picked.astype(BF16).reshape(HALF, 32, 256)

    pl.semaphore_wait(barrier, KPT - 1 + VIR - 1)

    def spread(kind, source, to):
        pair = to % HALF
        rows = pl.ds(pl.multiple_of((source // 4) * 32, 32), 32)
        slot = source % 4
        if kind == 0:
            return right.at[to // HALF, pair], far.at[slot, rows]
        return chunk.at[to], got.at[source]

    def spread_copy(kind, source, to):
        src, dst = spread(kind, source, to)
        return remote(src, dst, send_sem.at[kind, to], recv_sem.at[kind, source], (to, z))

    def own_spread(kind):
        src, dst = spread(kind, me, me)
        return pltpu.make_async_copy(src, dst, own_sem.at[kind])

    def spread_start(kind):
        loop(1, KPT, lambda i: spread_copy(kind, me, lax.rem(me + i, KPT)).start())
        own_spread(kind).start()

    def spread_recv(kind):
        loop(1, KPT, lambda i: spread_copy(kind, lax.rem(me + KPT - i, KPT), me).wait_recv())
        own_spread(kind).wait()

    def spread_sent(kind):
        loop(1, KPT, lambda i: spread_copy(kind, me, lax.rem(me + i, KPT)).wait_send())

    spread_start(0)

    line = y * 2 + core

    def slab_y(source, to):
        return remote(
            df_ref.at[pl.ds(0, 2), to], middle.at[:, source // 4, source % 4], slab_send.at[0, to], slab_recv.at[0, source],
            (x * 8 + to, z),
        )

    def slab_x(source, to):
        return remote(
            middle.at[to % 2], slab.at[pl.ds(2 * source, 2)], slab_send.at[1, to], slab_recv.at[1, source],
            (to * 8 + line, z),
        )

    own_y = pltpu.make_async_copy(df_ref.at[pl.ds(0, 2), line], middle.at[:, line // 4, line % 4], own_sem.at[2])
    own_x = pltpu.make_async_copy(middle.at[x % 2], slab.at[pl.ds(2 * x, 2)], own_sem.at[4])
    loop(1, 8, lambda i: slab_y(line, lax.rem(line + i, 8)).start())
    own_y.start()

    loads[1].wait()
    order = one_hot(
        128, 128, lambda n: bits(n, 6, 1) * 64 + bits(n, 0, 6)
    )
    lined = jnp.concatenate(
        [dot_rows(order, amp_ref[0, slot]).astype(BF16) for slot in range(4)], axis=0
    )
    to_owner = one_hot(
        512, 512,
        lambda n: bits(n, 2, 2) * 128 + bits(n, 0, 1) * 64 + bits(n, 4, 5) * 2 + bits(n, 1, 1),
    )
    chunk[...] = dot(to_owner, lined).astype(BF16).reshape(KPT, 16, 256)
    spread_start(1)

    def rest_copy(source, to):
        return remote(
            srest.at[to], mrest.at[source], rest_send.at[to], rest_recv.at[source], (me, to)
        )

    own_rest = pltpu.make_async_copy(srest.at[z], mrest.at[z], load_sem.at[3])
    loads[2].wait()

    @pl.when(half == 1)
    def _():
        rest = rest_ref[...].astype(F32)
        for tile in range(VIR):
            srest[tile] = rest[:, tile * 8 : tile * 8 + 8, :].reshape(64, 256).astype(BF16)
        loop(1, VIR, lambda i: rest_copy(z, lax.rem(z + i, VIR)).start())
        own_rest.start()

    turn = one_hot(256, 256, lambda n: bits(n, 0, 4) * 16 + bits(n, 4, 4))
    for slot in range(4):
        turned = dot(turn, amp_ref[1, slot]).astype(BF16)
        amps[spot_me, 4 + slot] = dot_rows(order, turned).astype(BF16)

    plan = (
        ((x, y), 0, 4, above), ((x, y), 0, 4, below), ((x, y), 0, 4, side),
        ((x_near, y), 0, 4, above), ((x_near, y), 0, 4, below),
        ((x, down), 0, 2, above), ((x, up), 2, 2, below), ((x, opposite), 0, 4, side),
    )
    arrive = (
        ((x, down), 0, 4), ((x, up), 0, 4), ((x_near, y), 0, 4),
        ((x_near, down), 0, 4), ((x_near, up), 0, 4),
        ((x, opposite), 0, 2), ((x, opposite), 2, 2), ((x_near, opposite), 0, 4),
        ((x, y), 0, 4),
    )

    def amp_copy(group, number):
        (xx, yy), low, count, device = plan[number]
        spot = amps.at[place(xx, yy, core), pl.ds(group * 4 + low, count)]
        return remote(spot, spot, amp_send.at[group, number], amp_recv.at[group, number], device)

    def amp_wait(group, number):
        (xx, yy), low, count = arrive[number]
        spot = amps.at[place(xx, yy, core), pl.ds(group * 4 + low, count)]
        remote(spot, spot, amp_send.at[group, number], amp_recv.at[group, number], mate).wait_recv()

    def mate_copy(group, number, whose):
        (xx, yy), low, count = arrive[number]
        spot = amps.at[place(xx, yy, whose), pl.ds(group * 4 + low, count)]
        return remote(spot, spot, mate_send.at[group, number], mate_recv.at[group, number], mate)

    def amp_begin(group):
        for number in (2, 0, 1):
            amp_copy(group, number).start()
        mate_copy(group, 8, core).start()

    def amp_steps(group, numbers, forward):
        for number in numbers:
            amp_wait(group, number)
        for number in forward:
            amp_copy(group, number).start()
        for number in numbers:
            mate_copy(group, number, core).start()

    amp_begin(1)

    column = lax.broadcasted_iota(jnp.int32, (64, 64), 1)
    diagonal = lax.broadcasted_iota(jnp.int32, (64, 64), 0) == column
    spread_vir = jnp.where(diagonal, jnp.broadcast_to(vir_ref[...].astype(F32), (64, 64)), 0.0)
    senergy[...] = dot(spread_vir.astype(BF16), jnp.ones((64, 128), BF16))
    energy_copy = remote(
        senergy, menergy, rest_send.at[VIR], rest_recv.at[VIR], (mirror, z)
    )
    energy_copy.start()

    spread_recv(0)
    eye = one_hot(256, 256, lambda n: n)
    for slot in range(4):
        turned = dot_rows(eye, far[pair_slot(slot)]).astype(BF16)
        tiles[z, slot] = jnp.where(slot < live_ref[0], turned, jnp.zeros_like(turned))

    def ring(way, hop, slot):
        held = lax.rem(z + (VIR - hop if way == 0 else hop), VIR)
        spot = tiles.at[held, slot]
        return remote(
            spot, spot, ring_send.at[way, hop, slot], ring_recv.at[way, hop, slot],
            ahead if way == 0 else behind,
        )

    def ring_wait(way, hop, slot):
        held = lax.rem(z + (VIR - hop - 1 if way == 0 else hop + 1), VIR)
        spot = tiles.at[held, slot]
        remote(
            spot, spot, ring_send.at[way, hop, slot], ring_recv.at[way, hop, slot],
            ahead if way == 0 else behind,
        ).wait_recv()

    def ways(hop, slot):
        if hop < 3:
            return (0, 1)
        return (0,) if slot < 2 else (1,)

    for slot in range(4):
        for way in (0, 1):
            ring(way, 0, slot).start()

    def ring_step(hop, slot):
        for way in ways(hop, slot):
            ring_wait(way, hop, slot)
        if hop < 3:
            for way in ways(hop + 1, slot):
                ring(way, hop + 1, slot).start()

    low = lax.broadcasted_iota(jnp.int32, (8, 8, 128), 2) < 64

    def couple(tile, slot):
        product = dot(tiles[tile, slot], slab[:, slot].reshape(256, 512)).reshape(8, 4, 8, 512)
        for pair in range(4):
            piece = product[..., pair * 128 : (pair + 1) * 128]
            evens, odds = [], []
            for first in (0, 2):
                here, there = piece[:, first], piece[:, first + 1]
                evens.append(jnp.where(low, here, pltpu.roll(there, 64, 2)))
                odds.append(jnp.where(low, pltpu.roll(here, 64, 2), there))
            block = jnp.concatenate(
                [jnp.concatenate(evens, axis=2), jnp.concatenate(odds, axis=2)], axis=1
            )
            block = block.astype(BF16)
            for run in range(8):
                coupled[slot, tile, pair * 16 : pair * 16 + 16, run * 256 : run * 256 + 256] = block[run]

    def couple_two(hop, slot):
        loop(0, 2, lambda i: couple(lax.rem(z + VIR + (2 * i - 1) * (hop + 1), VIR), slot))

    spread_recv(1)
    regroup = one_hot(
        512, 512,
        lambda n: bits(n, 1, 5) * 16 + bits(n, 7, 2) * 4 + bits(n, 6, 1) * 2 + bits(n, 0, 1),
    )
    regrouped = dot(regroup, got[...].reshape(512, 256)).astype(BF16)
    amps[spot_me, 0:4] = regrouped.reshape(4, 128, 256)
    amp_begin(0)

    loop(1, 8, lambda i: slab_y(lax.rem(line + 8 - i, 8), line).wait_recv())
    own_y.wait()
    for i in (2, 1, 3):
        slab_x(x, lax.rem(x + i, 4)).start()
    own_x.start()

    mover[...] = one_hot(512, 512, lambda n: bits(n, 0, 6) * 8 + bits(n, 6, 3))
    turner[...] = turn

    @pl.when(half == 1)
    def _():
        loop(1, VIR, lambda i: rest_copy(lax.rem(z + i, VIR), z).wait_recv())
        own_rest.wait()
        swapped = one_hot(
            512, 512, lambda n: bits(n, 6, 3) * 64 + bits(n, 0, 3) * 8 + bits(n, 3, 3)
        )
        moved = dot(swapped, mrest[...].reshape(512, 256)).astype(BF16)
        restored[...] = dot(moved, turner[...]).astype(BF16).reshape(VIR, 64, 256)

    ring_step(0, 0)
    ring_step(0, 1)
    ring_step(0, 2)
    ring_step(0, 3)
    amp_steps(1, (0, 1), (5, 6))
    amp_steps(1, (2,), (3, 4))
    ring_step(1, 0)
    amp_steps(0, (0, 1), (5, 6))
    amp_steps(0, (2,), (3, 4))
    ring_step(1, 1)
    ring_step(1, 2)
    ring_step(1, 3)
    amp_steps(1, (5, 6), (7,))
    ring_step(2, 0)
    loop(1, 4, lambda i: slab_x(lax.rem(x + 4 - i, 4), x).wait_recv())
    own_x.wait()
    loop(0, 4, lambda slot: couple(z, slot))
    couple_two(0, 0)
    couple_two(0, 1)
    ring_step(2, 1)
    amp_steps(0, (5, 6), (7,))
    couple_two(0, 2)
    couple_two(0, 3)
    ring_step(2, 2)
    couple_two(1, 0)
    couple_two(1, 1)
    ring_step(2, 3)
    couple_two(1, 2)
    couple_two(1, 3)
    amp_steps(1, (3, 4), ())
    amp_steps(0, (3, 4), ())
    couple_two(2, 0)
    couple_two(2, 1)
    ring_step(3, 0)
    ring_step(3, 2)
    couple_two(2, 2)
    couple(lax.rem(z + 4, VIR), 0)
    couple(lax.rem(z + 4, VIR), 2)
    couple_two(2, 3)
    ring_step(3, 1)
    ring_step(3, 3)
    couple(lax.rem(z + 4, VIR), 1)
    couple(lax.rem(z + 4, VIR), 3)
    amp_steps(1, (7,), ())
    amp_steps(0, (7,), ())
    for group in range(2):
        for number in range(9):
            mate_copy(group, number, 1 - core).wait_recv()

    for slot in range(4):
        both = amps[:, slot] + amps[:, 4 + pair_slot(slot)]
        summed_amps[slot] = both.reshape(2048, 256)

    def piece_copy(kind, source, to, device):
        return remote(
            part.at[to], shared.at[kind, source], swap_send.at[kind, to], swap_recv.at[kind, source],
            (device, to),
        )

    def pair_copy(pair):
        two = pl.ds(2 * pair, 2)
        return remote(
            whole.at[two], shared.at[0, two], swap_send.at[2, pair], swap_recv.at[2, pair], (mirror, z)
        )

    own_piece = pltpu.make_async_copy(part.at[z], shared.at[1, z], own_sem.at[3])

    def ladder(step):
        pair = lax.rem(z // 2 + jnp.where(step < 2, step + 2, 3 - step), 4)
        two = pl.ds(2 * pair, 2)
        partial = dot(coupled[0, two].reshape(128, 2048), summed_amps[0])
        for slot in range(1, 4):
            partial = partial + dot(coupled[slot, two].reshape(128, 2048), summed_amps[slot])
        total[two] = partial.reshape(2, 64, 256)

        @pl.when(half == 0)
        def _():
            rest = rest_ref[:, pl.ds(pl.multiple_of(pair * 16, 16), 16), :].astype(F32)
            for one in range(2):
                total[2 * pair + one] += rest[:, one * 8 : one * 8 + 8, :].reshape(64, 256)

        part[two] = total[two].astype(BF16)

        @pl.when(half == 0)
        def _():
            for one in range(2):
                piece_copy(0, z, 2 * pair + one, mirror).start()

        @pl.when(half == 1)
        def _():
            whole[two] = (total[two] + restored[two].astype(F32)).astype(BF16)
            pair_copy(pair).start()
            for one in range(2):
                to = 2 * pair + one

                @pl.when(to != z)
                def _():
                    piece_copy(1, z, to, me).start()

                @pl.when(to == z)
                def _():
                    own_piece.start()

    loop(0, 4, ladder)

    row = lax.broadcasted_iota(jnp.int32, (16, 256), 0)
    lane = lax.broadcasted_iota(jnp.int32, (16, 256), 1)
    occ_values = occ_ref[...]
    occ_first = dot(occ_values, jnp.where(lane // 16 == row, 1.0, 0.0).astype(BF16))
    occ_second = dot(occ_values, jnp.where(lane % 16 == row, 1.0, 0.0).astype(BF16))
    occ = jnp.where(
        half == 0, occ_first[0:1] + occ_second[1:2], occ_first[1:2] + occ_second[0:1]
    )
    energy_copy.wait_recv()

    def finish(own, flipped):
        summed = 0.0
        for block in flipped:
            moved = dot(mover[...], block.reshape(512, 256)).astype(BF16)
            summed = summed + dot(moved, turner[...])
        summed = summed.reshape(8, 64, 256) if flipped else None
        distant = jnp.concatenate([menergy[...]] * 2, axis=1)
        for v in range(8):
            near = jnp.concatenate([senergy[pl.ds(z * 8 + v, 1), :]] * 2, axis=1)
            out_ref[v] = ((own(v) if summed is None else own(v) + summed[v]) / (occ - near - distant)).astype(BF16)

    @pl.when(half == 0)
    def _():
        for pair in range(4):
            pair_copy(pair).wait_recv()

        def own(v):
            rows = slice(v * 8, v * 8 + 8)
            return (total[:, rows, :] + shared[0, :, rows, :].astype(F32)).reshape(64, 256)

        finish(own, ())
        loop(0, VIR, lambda i: piece_copy(0, z, lax.rem(z + i, VIR), mirror).wait_send())

    @pl.when(half == 1)
    def _():
        loop(0, VIR, lambda i: piece_copy(0, lax.rem(z + i, VIR), z, me).wait_recv())
        loop(1, VIR, lambda i: piece_copy(1, lax.rem(z + i, VIR), z, me).wait_recv())
        own_piece.wait()
        finish(lambda v: rest_ref[v].astype(F32), (shared[0], shared[1]))
        loop(1, VIR, lambda i: piece_copy(1, z, lax.rem(z + i, VIR), me).wait_send())
        for pair in range(4):
            pair_copy(pair).wait_send()
        loop(1, VIR, lambda i: rest_copy(z, lax.rem(z + i, VIR)).wait_send())

    for kind in range(2):
        spread_sent(kind)
    loop(1, 8, lambda i: slab_y(line, lax.rem(line + i, 8)).wait_send())
    loop(1, 4, lambda i: slab_x(x, lax.rem(x + i, 4)).wait_send())
    energy_copy.wait_send()
    for slot in range(4):
        for hop in range(4):
            for way in ways(hop, slot):
                ring(way, hop, slot).wait_send()
    for group in range(2):
        for number in range(8):
            amp_copy(group, number).wait_send()
        for number in range(9):
            mate_copy(group, number, core).wait_send()


def fused(slots, live, df, amp, rest, occ, vir):
    vmem = pl.BlockSpec(memory_space=pltpu.VMEM)
    smem = pl.BlockSpec(memory_space=pltpu.SMEM)
    hbm = pl.BlockSpec(memory_space=pl.ANY)
    dma = pltpu.SemaphoreType.DMA
    held = pltpu.VMEM
    return pl.pallas_call(
        fused_kernel,
        out_shape=jax.ShapeDtypeStruct((8, 64, 256), BF16),
        in_specs=[smem, smem, hbm, hbm, hbm, vmem, vmem],
        out_specs=vmem,
        scratch_shapes=[
            held((2, 8, 32, 512), BF16),
            held((2, 4, 256, 128), BF16),
            held((8, 64, 256), BF16),
            held((2, HALF, 32, 256), BF16),
            held((KPT, 16, 256), BF16),
            held((4, 256, 256), BF16),
            held((2, 2, 4, 32, 512), BF16),
            held((8, 4, 32, 512), BF16),
            held((KPT, 16, 256), BF16),
            held((VIR, 64, 256), BF16),
            held((VIR, 64, 256), BF16),
            held((64, 128), F32),
            held((64, 128), F32),
            held((VIR, 4, 256, 256), BF16),
            held((HALF, 8, 128, 256), BF16),
            held((4, VIR, 64, 2048), BF16),
            held((4, 2048, 256), BF16),
            held((VIR, 64, 256), F32),
            held((VIR, 64, 256), BF16),
            held((VIR, 64, 256), BF16),
            held((VIR, 64, 256), BF16),
            held((2, VIR, 64, 256), BF16),
            held((512, 512), BF16),
            held((256, 256), BF16),
            dma((5,)),
            dma((4,)),
            dma((2, KPT)),
            dma((2, KPT)),
            dma((2, 8)),
            dma((2, 8)),
            dma((VIR + 1,)),
            dma((VIR + 1,)),
            dma((2, 4, 4)),
            dma((2, 4, 4)),
            dma((2, 8)),
            dma((2, 8)),
            dma((2, 9)),
            dma((2, 9)),
            dma((3, VIR)),
            dma((3, VIR)),
        ],
        compiler_params=pltpu.CompilerParams(
            collective_id=0, has_side_effects=True, vmem_limit_bytes=56 * 1024 * 1024
        ),
        name="fused",
    )(slots, live, df, amp, rest, occ, vir)


def shards(df_pieces, amplitudes, rest_residual, occ_energy, vir_energy, live_slots, mirror_slot):
    out = fused(
        mirror_slot[0], live_slots, df_pieces.reshape(4, 8, 32, 512), amplitudes, rest_residual[0],
        occ_energy, vir_energy,
    )
    return out[None]


def solution(mesh):
    placed = (
        P("kpt", None, None, "vir"),
        P(None, None, None, "kpt"),
        P("kpt", "vir", None, None),
        P(),
        P("kpt", None),
        P("kpt"),
        P("kpt", None),
    )
    return jax.shard_map(
        shards, mesh=mesh, in_specs=placed, out_specs=P("kpt", "vir", None, None), check_vma=False
    )
```
